512 devices in a mesh: slab: 8 (over z_hi, core), dom: 64 (over y, x, z_lo).
Axes of the slice: x: 4, y: 8, z: 8 (z_hi: 4, z_lo: 2; z = z_hi * 2 + z_lo), core: 2. Of those that a mesh axis runs over, the one named last changes fastest.
Arguments:
- particles: bfloat16 [2048, 256, 2, 128], P(('slab', 'dom')), may hold values from -6 to 6
- defocus: float32 [2048], P(('slab', 'dom')), may hold values from 8000 to 30000
- inverse_noise: float32 [2048], P(('slab', 'dom')), may hold values from 0.002 to 0.05
- volume: bfloat16 [2, 33554432], P(None, ('slab', 'dom')), may hold values from -6 to 6
- slice_owner: int32 [8, 256], replicated, may hold values from 0 to 511, as said below
- slice_voxel: int32 [8, 256, 128], replicated, may hold values from 0 to 65535
Outputs:
- back_projection: float32 [2, 33554432], P(None, ('slab', 'dom'))
The draws below stay inside these ranges and needn't reach their ends.
Inputs may be any that keep to these rules, and one draw needn't show every extreme that they name: `slice_owner`: no device owns more than 6 slice rows, and some device owns exactly 6.
All inputs are finite; a program needn't handle non-finite values.
Results may differ from the reference program's by a relative error of at most 0.005.
Values may be sent and summed in bfloat16 or wider, within the bound.
No kernel may reach another device: no remote copies, remote signals or barrier semaphores. Data moves between devices by JAX's collectives and lax.ppermute only.
A program may use at most 128 MiB of HBM per device.

```python
import math
import jax
import jax.numpy as jnp
from jax import lax

KY = 256
KX = 128
REFS = 8
SHIFTS = 32
VOX_DEV = 65536
CAP = 6
PARTICLES = 2048
VOXELS = 33554432
DEVICES = 512


def draw_slice_owner(key, part):
    key = jax.random.fold_in(key, 11)
    key_order, key_full, key_rows = jax.random.split(key, 3)
    slot_total = DEVICES * CAP
    order = jax.random.permutation(key_order, slot_total)
    position = jnp.argsort(order)
    full_device = jax.random.randint(key_full, (), 0, DEVICES)
    slot_ids = jnp.arange(slot_total, dtype=jnp.int32)
    priority = jnp.where(slot_ids // CAP == full_device, slot_ids - slot_total, position.astype(jnp.int32))
    chosen = jnp.argsort(priority)[:REFS * KY]
    chosen = jax.random.permutation(key_rows, chosen)
    return (chosen // CAP).reshape(REFS, KY).astype(jnp.int32)


def draw_volume(key, part):
    key = jax.random.fold_in(key, 23)
    key_phase = jax.random.fold_in(key, 0)
    values = jnp.clip(jax.random.normal(key_phase, (2, VOXELS), jnp.float32), -6.0, 6.0)
    return values.astype(jnp.bfloat16)


def place_ends(result, own_key, smallest, high):
    shape = result.shape
    place = [jax.random.randint(jax.random.fold_in(own_key, axis), (), 0, shape[axis]) for axis in range(len(shape))]
    result = result.at[tuple(place)].set(smallest)
    longest = shape.index(max(shape))
    place[longest] = (place[longest] + 1) % shape[longest]
    return result.at[tuple(place)].set(high)


def shard_levels(rng, extent, cuts, least, high):
    def one(dim, shards_of):
        draws = jax.random.uniform(jax.random.fold_in(jax.random.fold_in(rng, 6), dim), (shards_of,), jnp.float32, least / len(cuts), high / len(cuts))
        return jnp.repeat(jnp.exp(draws), extent[dim] // shards_of).reshape((-1,) + (1,) * (len(extent) - dim - 1))

    gain = one(*cuts[0])
    for cut in cuts[1:]:
        gain = gain * one(*cut)
    return gain


def centred(stream_key, extent, deviation, reach, shards=(), kind=jnp.bfloat16):
    array = jax.random.normal(stream_key, extent, jnp.float32) * deviation
    if len(shards) > 0:
        array = shard_levels(stream_key, extent, shards, -0.22, 0.18) * array
    return jnp.clip(array, min=-reach, max=reach).astype(kind)


def setup_inputs(seed: int = 0) -> dict:
    seeds = jax.random.split(jax.random.key(seed), 7)
    particles = centred(seeds[0], (PARTICLES, KY, 2, KX), 1.0, 6.0, ((0, 512),))
    defocus = jnp.clip(8000.0 + 22000.0 * jax.random.uniform(seeds[1], (PARTICLES,), jnp.float32) ** shard_levels(seeds[1], (PARTICLES,), ((0, 512),), -0.2, 0.2), 8000.0, 30000.0)
    inverse_noise = jnp.clip(jnp.exp(math.log(0.05) - 3.218876 * jax.random.uniform(seeds[2], (PARTICLES,), jnp.float32) ** shard_levels(seeds[2], (PARTICLES,), ((0, 512),), -0.2, 0.2)), 0.002, 0.05)
    volume = draw_volume(jax.random.fold_in(seeds[6], 71), 0)
    slice_owner = draw_slice_owner(jax.random.fold_in(seeds[6], 71), 0)
    slice_voxel = place_ends(jax.random.randint(seeds[5], (REFS, KY, KX), 0, VOX_DEV), jax.random.fold_in(seeds[5], 1), 0, VOX_DEV - 1).astype(jnp.int32)
    return dict(particles=particles, defocus=defocus, inverse_noise=inverse_noise, volume=volume, slice_owner=slice_owner, slice_voxel=slice_voxel)


box_edge = 400
wavelength = 0.0197
amp_contrast = 0.1

def contrast_transfer(defocus_value, ky_count, kx_count):
    freq_y = (jnp.arange(ky_count, dtype=jnp.int32) - ky_count // 2).astype(jnp.float32)
    freq_x = jnp.arange(kx_count, dtype=jnp.int32).astype(jnp.float32)
    radius_sq = (freq_y[:, None] * freq_y[:, None] + freq_x[None, :] * freq_x[None, :]) / (box_edge * box_edge)
    chi_angle = math.pi * wavelength * defocus_value * radius_sq
    return -(math.sqrt(0.99) * jnp.sin(chi_angle) + amp_contrast * jnp.cos(chi_angle))

def phase_tables(ky_count, kx_count, shift_count):
    shift_vals = jnp.arange(shift_count, dtype=jnp.int32) - shift_count // 2
    freq_y = jnp.arange(ky_count, dtype=jnp.int32) - ky_count // 2
    freq_x = jnp.arange(kx_count, dtype=jnp.int32)
    angle_y = 2.0 * math.pi / box_edge * jnp.mod(freq_y[:, None] * shift_vals[None, :], box_edge).astype(jnp.float32)
    angle_x = 2.0 * math.pi / box_edge * jnp.mod(freq_x[:, None] * shift_vals[None, :], box_edge).astype(jnp.float32)
    cos_y = jnp.cos(angle_y).astype(jnp.bfloat16)
    sin_y = jnp.sin(angle_y).astype(jnp.bfloat16)
    cos_x = jnp.cos(angle_x).astype(jnp.bfloat16)
    sin_x = jnp.sin(angle_x).astype(jnp.bfloat16)
    forward_x = jnp.concatenate([jnp.concatenate([cos_x, sin_x], axis=1), jnp.concatenate([-sin_x, cos_x], axis=1)], axis=0)
    backward_x = jnp.concatenate([jnp.concatenate([cos_x.T, sin_x.T], axis=1), jnp.concatenate([-sin_x.T, cos_x.T], axis=1)], axis=0)
    corr_y = jnp.concatenate([cos_y.T, -sin_y.T], axis=1)
    back_y = jnp.concatenate([cos_y, sin_y], axis=0)
    return (forward_x, backward_x, corr_y, back_y)

def particle_term(image, defocus_value, noise_scale, slices, tables):
    forward_x, backward_x, corr_y, back_y = tables
    ref_count, ky_count, _, kx_count = slices.shape
    shift_count = corr_y.shape[0]
    ctf_values = contrast_transfer(defocus_value, ky_count, kx_count)
    image_f = image.astype(jnp.float32)
    image_re = image_f[:, 0, :]
    image_im = image_f[:, 1, :]
    slice_f = slices.astype(jnp.float32)
    slice_re = slice_f[:, :, 0, :]
    slice_im = slice_f[:, :, 1, :]
    q_re = ctf_values * (slice_re * image_re + slice_im * image_im)
    q_im = ctf_values * (slice_re * image_im - slice_im * image_re)
    q_all = jnp.stack([q_re, q_im], axis=2).astype(jnp.bfloat16)
    row_phase = jnp.dot(q_all.reshape(ref_count * ky_count, 2 * kx_count), forward_x, preferred_element_type=jnp.float32)
    row_phase = row_phase.astype(jnp.bfloat16).reshape(ref_count, ky_count, 2, shift_count)
    row_phase = jnp.transpose(row_phase, (0, 2, 1, 3)).reshape(ref_count, 2 * ky_count, shift_count)
    corr = jnp.einsum('ik,rkj->rij', corr_y.astype(jnp.float32), row_phase.astype(jnp.float32))
    power = lax.optimization_barrier(jnp.sum((ctf_values * ctf_values)[None] * (slice_re * slice_re + slice_im * slice_im), axis=(1, 2)))
    score = noise_scale * (corr - 0.5 * power[:, None, None])
    weight = jax.nn.softmax(score.reshape(-1)).reshape(score.shape).astype(jnp.bfloat16)
    col_phase = jnp.einsum('ki,rij->rkj', back_y.astype(jnp.float32), weight.astype(jnp.float32)).astype(jnp.bfloat16)
    col_phase = jnp.transpose(col_phase.reshape(ref_count, 2, ky_count, shift_count), (0, 2, 1, 3))
    shift_sum = jnp.dot(col_phase.reshape(ref_count * ky_count, 2 * shift_count), backward_x, preferred_element_type=jnp.float32)
    shift_sum = shift_sum.astype(jnp.bfloat16).astype(jnp.float32).reshape(ref_count, ky_count, 2, kx_count)
    sum_re = shift_sum[:, :, 0, :]
    sum_im = shift_sum[:, :, 1, :]
    term_re = ctf_values * (image_re * sum_re - image_im * sum_im)
    term_im = ctf_values * (image_re * sum_im + image_im * sum_re)
    return jnp.stack([term_re, term_im], axis=2)

def reference(particles, defocus, inverse_noise, volume, slice_owner, slice_voxel):
    global_index = (slice_owner[:, :, None] * VOX_DEV + slice_voxel).astype(jnp.int32)
    slices = jnp.stack([volume[0][global_index], volume[1][global_index]], axis=2)
    tables = phase_tables(KY, KX, SHIFTS)

    def accumulate(total, item):
        image, defocus_value, noise_scale = item
        return (total + particle_term(image, defocus_value, noise_scale, slices, tables), None)
    start = jnp.zeros((REFS, KY, 2, KX), jnp.float32)
    inserted, _ = lax.scan(accumulate, start, (particles, defocus, inverse_noise))
    moved = jnp.moveaxis(inserted, 2, 0)
    added = jnp.zeros((2, VOXELS), jnp.float32).at[:, global_index].add(moved)
    return added / math.sqrt(PARTICLES)
```

```python
import math

import jax
import jax.numpy as jnp
import ml_dtypes
import numpy as np
from jax import lax
from jax.experimental import pallas as pl
from jax.experimental.pallas import tpu as pltpu
from jax.sharding import Mesh
from jax.sharding import PartitionSpec as P

KY, KX, REFS, SHIFTS, CAP, PER = 256, 128, 8, 32, 6, 4
ROWS = REFS * KY
PARTICLES = 2048
HALF = 1536
BOX = 400
WAVE = 0.0197
AMP = 0.1
VMEM_LIMIT = 40 * 1024 * 1024
FINE = ("zh", "c", "y", "x", "zl")
F32 = jnp.float32
BF16 = jnp.bfloat16


def phase_constants():
    shift = np.arange(SHIFTS) - SHIFTS // 2
    fy = np.arange(KY) - KY // 2
    fx = np.arange(KX)
    ang_y = 2.0 * np.pi / BOX * np.mod(fy[:, None] * shift[None, :], BOX)
    ang_x = 2.0 * np.pi / BOX * np.mod(fx[:, None] * shift[None, :], BOX)
    cos_y, sin_y, cos_x, sin_x = np.cos(ang_y), np.sin(ang_y), np.cos(ang_x), np.sin(ang_x)
    fwd = np.zeros((PER, 2, KX, 2, PER, SHIFTS))
    bwd = np.zeros((2, PER, SHIFTS, PER, 2, KX))
    for p in range(PER):
        fwd[p, 0, :, 0, p], fwd[p, 0, :, 1, p] = cos_x, sin_x
        fwd[p, 1, :, 0, p], fwd[p, 1, :, 1, p] = -sin_x, cos_x
        bwd[0, p, :, p, 0], bwd[0, p, :, p, 1] = cos_x.T, sin_x.T
        bwd[1, p, :, p, 0], bwd[1, p, :, p, 1] = -sin_x.T, cos_x.T
    fwd = fwd.reshape(PER * 2 * KX, 2 * PER * SHIFTS)
    bwd = bwd.reshape(2 * PER * SHIFTS, PER * 2 * KX)
    corr = np.concatenate([cos_y.T, sin_y.T], axis=0)
    back = np.concatenate([cos_y, sin_y], axis=0)
    return [a.astype(np.float32).astype(ml_dtypes.bfloat16) for a in (fwd, bwd, corr, back)]


def iota(shape, dim):
    return lax.broadcasted_iota(jnp.int32, shape, dim)


def pick_kernel(me_ref, own_ref, own_t_ref, vol_ref, vox_ref, pos_ref, mine_ref, out_ref, slot, stage):
    me = me_ref[0]
    blocks = ROWS // 128
    cols = [jnp.broadcast_to(own_t_ref[:, c : c + 1], (128, 128)) for c in range(blocks)]
    earlier = iota((128, 128), 0) < iota((128, 128), 1)
    for b in range(blocks):
        here = jnp.broadcast_to(own_ref[b : b + 1, :], (128, 128))
        hits = ((cols[b] == here) & earlier).astype(F32)
        for c in range(b):
            hits = hits + (cols[c] == here).astype(F32)
        slot[b : b + 1, :] = jnp.sum(hits, axis=0, keepdims=True).astype(jnp.int32)
    own = own_ref[...]
    slots = slot[...]
    g1 = lax.shift_right_logical(own, 7) * 2 + (own & 1)
    g2 = (lax.shift_right_logical(own, 3) & 7) * 4 + (lax.shift_right_logical(own, 1) & 3)
    across = ((lax.shift_right_logical(own, 6) ^ lax.shift_right_logical(me, 6)) & 1) * HALF
    pos_ref[...] = across + g2 * 48 + g1 * CAP + jnp.minimum(slots, CAP - 1)
    row_id = iota((blocks, 128), 0) * 128 + iota((blocks, 128), 1)
    is_me = own == me
    table = vol_ref[...]
    parity = (iota((8, 128), 0) & 1) == 0
    row_pair = lax.shift_right_logical(iota((1024, 128), 0), 1)
    lo_iota = iota((128, 128), 0)
    mine_ref[...] = jnp.full((8, 128), -1, jnp.int32)
    for k in range(CAP):
        hit = is_me & (slots == k)
        row = jnp.max(jnp.where(hit, row_id, -1))
        vox = vox_ref[pl.ds(jnp.maximum(row, 0), 1), :]
        vox = jnp.where(row >= 0, vox, -1)
        mine_ref[k : k + 1, :] = vox
        hi = lax.shift_right_arithmetic(vox, 7)
        onehot = (lo_iota == (vox & 127)).astype(F32).astype(BF16)
        wide = jnp.dot(table, onehot, preferred_element_type=F32)
        kept = jnp.where(row_pair == hi, wide, 0.0)
        kept = jnp.sum(kept.reshape(128, 8, 128), axis=0)
        re = jnp.sum(jnp.where(parity, kept, 0.0), axis=0, keepdims=True)
        im = jnp.sum(jnp.where(parity, 0.0, kept), axis=0, keepdims=True)
        for copy in range(8):
            stage[copy * 12 + 2 * k : copy * 12 + 2 * k + 1, :] = re
            stage[copy * 12 + 2 * k + 1 : copy * 12 + 2 * k + 2, :] = im
    out_ref[...] = stage[...].astype(BF16)


def image_kernel(defocus_ref, part_ref, img_ref, sq_ref, wide):
    fy = (iota((KY, KX), 0) - KY // 2).astype(F32)
    fx = iota((KY, KX), 1).astype(F32)
    radius = (fy * fy + fx * fx) / float(BOX * BOX)
    phase0 = math.asin(AMP)
    pi_a = 3.140625
    pi_b = 9.67502593994140625e-4
    pi_c = math.pi - pi_a - pi_b
    coef = [(-1.0) ** k / math.factorial(2 * k + 1) for k in range(7)]
    for p in range(PER):
        wide[...] = part_ref[p * 512 : (p + 1) * 512, :].astype(F32)
        chi = (math.pi * WAVE * defocus_ref[p]) * radius
        whole = jnp.floor(chi * (1.0 / math.pi) + (phase0 / math.pi + 0.5))
        frac = ((chi - whole * pi_a) - whole * pi_b) - (whole * pi_c - phase0)
        half = whole * 0.5
        frac = frac * (1.0 - 4.0 * (half - jnp.floor(half)))
        sq = frac * frac
        poly = jnp.full_like(sq, coef[6])
        for k in range(5, -1, -1):
            poly = poly * sq + coef[k]
        ctf = -(poly * frac)
        sq_ref[p * KY : (p + 1) * KY, :] = ctf * ctf
        img_ref[p * 512 : p * 512 + KY, :] = ctf * wide[pl.ds(0, KY, stride=2), :]
        img_ref[p * 512 + KY : (p + 1) * 512, :] = ctf * wide[pl.ds(1, KY, stride=2), :]


CH = 64


def search_kernel(pos_ref, noise_ref, near_ref, far_ref, img_ref, sq_ref, fwd_ref, bwd_ref, corr_ref, back_ref,
                  sum_ref, far_out_ref, slots, rows, q, power, corr, weight):
    slots[0 : 2 * HALF, :] = near_ref[...].astype(F32)
    slots[2 * HALF : 4 * HALF, :] = far_ref[...].astype(F32)
    sum_ref[...] = jnp.zeros_like(sum_ref)

    def forward(r, carry):
        def fetch(g, c):
            for u in range(32):
                y = g * 32 + u
                at = pl.multiple_of(2 * pos_ref[r * KY + y], 2)
                rows[pl.ds(pl.multiple_of(2 * y, 2), 2), :] = slots[pl.ds(at, 2), :]
            return c

        lax.fori_loop(0, KY // 32, fetch, 0)
        sums = [jnp.zeros((8, KX), F32) for _ in range(PER)]
        for k in range(KY // CH):
            re = rows[pl.ds(2 * CH * k, CH, stride=2), :]
            im = rows[pl.ds(2 * CH * k + 1, CH, stride=2), :]
            mag = re * re + im * im
            for p in range(PER):
                a_re = img_ref[p * 512 + k * CH : p * 512 + (k + 1) * CH, :]
                a_im = img_ref[p * 512 + KY + k * CH : p * 512 + KY + (k + 1) * CH, :]
                q[k * CH : (k + 1) * CH, p * 256 : p * 256 + 128] = (re * a_re + im * a_im).astype(BF16)
                q[k * CH : (k + 1) * CH, p * 256 + 128 : (p + 1) * 256] = (re * a_im - im * a_re).astype(BF16)
                part = sq_ref[p * KY + k * CH : p * KY + (k + 1) * CH, :] * mag
                sums[p] = sums[p] + jnp.sum(part.reshape(CH // 8, 8, KX), axis=0)
        for p in range(PER):
            power[pl.ds(p * REFS + r, 1), :] = jnp.sum(sums[p], axis=0, keepdims=True)
        row_phase = jnp.dot(q[...], fwd_ref[...], preferred_element_type=F32).astype(BF16)
        both = jnp.dot(corr_ref[...], row_phase, preferred_element_type=F32)
        corr[pl.ds(pl.multiple_of(r * SHIFTS, SHIFTS), SHIFTS), :] = both[:SHIFTS, :128] - both[SHIFTS:, 128:]
        return carry

    lax.fori_loop(0, REFS, forward, 0)

    group = lax.shift_right_logical(iota((1, 128), 1), 5)
    noise = jnp.zeros((1, 128), F32)
    totals = jnp.zeros((REFS, 128), F32)
    for p in range(PER):
        noise = jnp.where(group == p, noise_ref[p], noise)
        column = jnp.sum(power[p * REFS : (p + 1) * REFS, :], axis=1, keepdims=True)
        totals = jnp.where(group == p, column, totals)
    score = corr[...].reshape(REFS, SHIFTS, 128) - 0.5 * totals[:, None, :]
    score = score.reshape(REFS * SHIFTS, 128) * noise
    top = jnp.max(score, axis=0, keepdims=True)
    peak = jnp.zeros((1, 128), F32)
    for p in range(PER):
        peak = jnp.where(group == p, jnp.max(jnp.where(group == p, top, -jnp.inf), axis=1, keepdims=True), peak)
    expo = jnp.exp(score - peak)
    lane_sum = jnp.sum(expo, axis=0, keepdims=True)
    norm = jnp.ones((1, 128), F32)
    for p in range(PER):
        norm = jnp.where(group == p, jnp.sum(jnp.where(group == p, lane_sum, 0.0), axis=1, keepdims=True), norm)
    weight[...] = (expo * (1.0 / norm)).astype(BF16)

    def backward(r, carry):
        w = weight[pl.ds(pl.multiple_of(r * SHIFTS, SHIFTS), SHIFTS), :]
        col = jnp.dot(back_ref[...], w, preferred_element_type=F32).astype(BF16)
        col = jnp.concatenate([col[:KY], col[KY:]], axis=1)
        for k in range(KY // CH):
            ss = jnp.dot(col[k * CH : (k + 1) * CH], bwd_ref[...], preferred_element_type=F32).astype(BF16).astype(F32)
            t_re = t_im = None
            for p in range(PER):
                a_re = img_ref[p * 512 + k * CH : p * 512 + (k + 1) * CH, :]
                a_im = img_ref[p * 512 + KY + k * CH : p * 512 + KY + (k + 1) * CH, :]
                s_re = ss[:, p * 256 : p * 256 + 128]
                s_im = ss[:, p * 256 + 128 : (p + 1) * 256]
                u_re = a_re * s_re - a_im * s_im
                u_im = a_re * s_im + a_im * s_re
                t_re = u_re if t_re is None else t_re + u_re
                t_im = u_im if t_im is None else t_im + u_im
            rows[pl.ds(2 * CH * k, CH, stride=2), :] = t_re
            rows[pl.ds(2 * CH * k + 1, CH, stride=2), :] = t_im

        def put(g, c):
            for u in range(32):
                y = g * 32 + u
                at = pl.multiple_of(2 * pos_ref[r * KY + y], 2)
                sum_ref[pl.ds(at, 2), :] = rows[pl.ds(pl.multiple_of(2 * y, 2), 2), :]
            return c

        lax.fori_loop(0, KY // 32, put, 0)
        return carry

    lax.fori_loop(0, REFS, backward, 0)
    far_out_ref[...] = sum_ref[2 * HALF : 4 * HALF, :].astype(BF16)


def insert_kernel(mine_ref, got_ref, out_ref, wide, left, right):
    wide[...] = got_ref[...].astype(F32)
    scale = 1.0 / math.sqrt(PARTICLES)
    hi_iota = iota((512, 128), 0)
    lo_iota = iota((128, 128), 0)
    for k in range(CAP):
        vox = mine_ref[k : k + 1, :]
        hi = lax.shift_right_arithmetic(vox, 7)
        onehot = (lo_iota == (vox & 127)).astype(F32).astype(BF16)
        right[:, 2 * k * 128 : (2 * k + 1) * 128] = onehot
        right[:, (2 * k + 1) * 128 : (2 * k + 2) * 128] = onehot
        at = hi_iota == hi
        for c in range(2):
            total = jnp.zeros((1, 128), F32)
            for src in range(8):
                total = total + wide[src * 12 + 2 * k + c : src * 12 + 2 * k + c + 1, :]
            total = total * scale
            first = total.astype(BF16).astype(F32)
            rest = total - first
            left[c, :, 2 * k * 128 : (2 * k + 1) * 128] = jnp.where(at, first, 0.0).astype(BF16)
            left[c, :, (2 * k + 1) * 128 : (2 * k + 2) * 128] = jnp.where(at, rest, 0.0).astype(BF16)
    for c in range(2):
        out_ref[pl.ds(c, 512, stride=2), :] = lax.dot_general(
            left[c], right[...], (((1,), (1,)), ((), ())), preferred_element_type=F32
        )


VM = pl.BlockSpec(memory_space=pltpu.VMEM)
SM = pl.BlockSpec(memory_space=pltpu.SMEM)


def shape(dims, dtype):
    return jax.ShapeDtypeStruct(dims, dtype)


def params():
    return pltpu.CompilerParams(vmem_limit_bytes=VMEM_LIMIT)


def cost(us):
    return pl.CostEstimate(flops=int(us * 1e9), bytes_accessed=int(us * 1e6), transcendentals=0)


def pick_call(me, owner, volume_rows, voxel_rows):
    own = owner.reshape(ROWS // 128, 128)
    return pl.pallas_call(
        pick_kernel,
        out_shape=(
            shape((ROWS // 128, 128), jnp.int32),
            shape((8, 128), jnp.int32),
            shape((8 * 12, 128), BF16),
        ),
        in_specs=[SM, VM, VM, VM, VM],
        out_specs=(VM, VM, VM),
        scratch_shapes=[pltpu.VMEM((ROWS // 128, 128), jnp.int32), pltpu.VMEM((96, 128), F32)],
        compiler_params=params(),
        name="pick_rows",
    )(me, own, own.T, volume_rows, voxel_rows)


def image_call(defocus, particle_rows):
    return pl.pallas_call(
        image_kernel,
        out_shape=(shape((PER * 512, KX), F32), shape((PER * KY, KX), F32)),
        in_specs=[SM, VM],
        out_specs=(VM, VM),
        scratch_shapes=[pltpu.VMEM((512, KX), F32)],
        compiler_params=params(),
        cost_estimate=cost(4),
        name="ctf_images",
    )(defocus, particle_rows)


def search_call(pos, noise, near, far, img, sq):
    tables = [jnp.asarray(t) for t in phase_constants()]
    return pl.pallas_call(
        search_kernel,
        out_shape=(shape((4 * HALF, KX), F32), shape((2 * HALF, KX), BF16)),
        in_specs=[SM, SM] + [VM] * 8,
        out_specs=(VM, VM),
        scratch_shapes=[
            pltpu.VMEM((4 * HALF, KX), F32),
            pltpu.VMEM((2 * KY, KX), F32),
            pltpu.VMEM((KY, PER * 2 * KX), BF16),
            pltpu.VMEM((PER * REFS, KX), F32),
            pltpu.VMEM((REFS * SHIFTS, 128), F32),
            pltpu.VMEM((REFS * SHIFTS, 128), BF16),
        ],
        compiler_params=params(),
        name="shift_search",
    )(pos, noise, near, far, img, sq, *tables)


def insert_call(mine, got):
    return pl.pallas_call(
        insert_kernel,
        out_shape=shape((1024, 128), F32),
        in_specs=[VM, VM],
        out_specs=VM,
        scratch_shapes=[
            pltpu.VMEM((96, 128), F32),
            pltpu.VMEM((2, 512, 2 * CAP * 128), BF16),
            pltpu.VMEM((128, 2 * CAP * 128), BF16),
        ],
        compiler_params=params(),
        name="insert_rows",
    )(mine, got)


def local(particles, defocus, inverse_noise, volume, slice_owner, slice_voxel):
    me = lax.axis_index(FINE).astype(jnp.int32).reshape(1)
    volume_rows = volume.reshape(2, 512, 128).transpose(1, 0, 2).reshape(1024, 128)
    pos, mine, compact = pick_call(me, slice_owner, volume_rows, slice_voxel.reshape(ROWS, KX))
    pos = pos.reshape(ROWS)
    line = lax.all_to_all(compact.reshape(8, CAP, 2, 128), ("zh", "zl"), 0, 0, tiled=True)
    spread = jnp.broadcast_to(line.reshape(1, 48, 2, 128), (32, 48, 2, 128))
    near = lax.all_to_all(spread, ("y", "x"), 0, 0, tiled=True).reshape(HALF, 2, 128)
    swap = [(0, 1), (1, 0)]
    far = lax.ppermute(near, "c", swap)
    img, sq = image_call(defocus, particles.reshape(PER * KY * 2, KX))
    sums, far_out = search_call(
        pos, inverse_noise, near.reshape(2 * HALF, 128), far.reshape(2 * HALF, 128), img, sq
    )
    received = lax.ppermute(far_out.reshape(HALF, 2, 128), "c", swap)
    pair = sums[: 2 * HALF].reshape(HALF, 2, 128) + received.astype(F32)
    plane = lax.all_to_all(pair.astype(BF16).reshape(32, 48, 2, 128), ("y", "x"), 0, 0, tiled=True)
    plane = jnp.sum(plane.astype(F32), axis=0).astype(BF16)
    last = lax.all_to_all(plane.reshape(8, CAP, 2, 128), ("zh", "zl"), 0, 0, tiled=True)
    out = insert_call(mine, last.reshape(96, 128))
    return out.reshape(512, 2, 128).transpose(1, 0, 2).reshape(2, 65536)


def solution(mesh):
    fine = Mesh(mesh.devices.reshape(4, 2, 8, 4, 2), FINE)
    in_specs = (P(FINE, None, None, None), P(FINE), P(FINE), P(None, FINE), P(), P())
    return jax.shard_map(local, mesh=fine, in_specs=in_specs, out_specs=P(None, FINE), check_vma=False)
```

```python
import math

import jax
import jax.numpy as jnp
import ml_dtypes
import numpy as np
from jax import lax
from jax.experimental import pallas as pl
from jax.experimental.pallas import tpu as pltpu
from jax.sharding import Mesh
from jax.sharding import PartitionSpec as P

KY, KX, REFS, SHIFTS, CAP, PER = 256, 128, 8, 32, 6, 4
ROWS = REFS * KY
PARTICLES = 2048
HALF = 1536
BOX = 400
WAVE = 0.0197
AMP = 0.1
VMEM_LIMIT = 40 * 1024 * 1024
FINE = ("zh", "c", "y", "x", "zl")
F32 = jnp.float32
BF16 = jnp.bfloat16


def phase_constants():
    shift = np.arange(SHIFTS) - SHIFTS // 2
    fy = np.arange(KY) - KY // 2
    fx = np.arange(KX)
    ang_y = 2.0 * np.pi / BOX * np.mod(fy[:, None] * shift[None, :], BOX)
    ang_x = 2.0 * np.pi / BOX * np.mod(fx[:, None] * shift[None, :], BOX)
    cos_y, sin_y, cos_x, sin_x = np.cos(ang_y), np.sin(ang_y), np.cos(ang_x), np.sin(ang_x)
    fwd = np.zeros((PER, 2, KX, 2, PER, SHIFTS))
    bwd = np.zeros((2, PER, SHIFTS, PER, 2, KX))
    for p in range(PER):
        fwd[p, 0, :, 0, p], fwd[p, 0, :, 1, p] = cos_x, sin_x
        fwd[p, 1, :, 0, p], fwd[p, 1, :, 1, p] = -sin_x, cos_x
        bwd[0, p, :, p, 0], bwd[0, p, :, p, 1] = cos_x.T, sin_x.T
        bwd[1, p, :, p, 0], bwd[1, p, :, p, 1] = -sin_x.T, cos_x.T
    fwd = fwd.reshape(PER * 2 * KX, 2 * PER * SHIFTS)
    bwd = bwd.reshape(2 * PER * SHIFTS, PER * 2 * KX)
    corr = np.concatenate([cos_y.T, sin_y.T], axis=0)
    back = np.concatenate([cos_y, sin_y], axis=0)
    return [a.astype(np.float32).astype(ml_dtypes.bfloat16) for a in (fwd, bwd, corr, back)]


def iota(shape, dim):
    return lax.broadcasted_iota(jnp.int32, shape, dim)


def pick_kernel(me_ref, own_ref, vol_hbm, vox_hbm, pos_ref, mine_ref, out_ref, slot, stage, table, near_rows, sems):
    load = pltpu.make_async_copy(vol_hbm, table, sems.at[CAP])
    load.start()
    me = me_ref[0]
    own = own_ref[...]
    turned = own.astype(F32).T
    cols, here = [], []
    for b in range(ROWS // 128):
        r, h = b // 2, b % 2
        cols.append(jnp.broadcast_to(turned[h * 128 : (h + 1) * 128, r : r + 1], (128, 128)))
        here.append(jnp.broadcast_to(own[r : r + 1, h * 128 : (h + 1) * 128].astype(F32), (128, 128)))
    earlier = iota((128, 128), 0) < iota((128, 128), 1)
    for b in range(ROWS // 128):
        r, h = b // 2, b % 2
        hits = ((cols[b] == here[b]) & earlier).astype(F32)
        for c in range(b):
            hits = hits + (cols[c] == here[b]).astype(F32)
        slot[r : r + 1, h * 128 : (h + 1) * 128] = jnp.sum(hits, axis=0, keepdims=True).astype(jnp.int32)
    slots = slot[...]
    row_id = iota((REFS, KY), 0) * KY + iota((REFS, KY), 1)
    is_me = own == me
    found, loads = [], []
    for k in range(CAP):
        row = jnp.max(jnp.where(is_me & (slots == k), row_id, -1))
        start = pl.multiple_of(jnp.maximum(row, 0) // 8 * 8, 8)
        found.append(row)
        loads.append(pltpu.make_async_copy(vox_hbm.at[pl.ds(start, 8), :], near_rows.at[k], sems.at[k]))
        loads[k].start()
    z = lax.shift_right_logical(own, 7) * 2 + (own & 1)
    y = lax.shift_right_logical(own, 3) & 7
    x = lax.shift_right_logical(own, 1) & 3
    across = ((lax.shift_right_logical(own, 6) ^ lax.shift_right_logical(me, 6)) & 1) * HALF
    pos_ref[...] = 2 * (across + x * (64 * CAP) + (z * 8 + y) * CAP + jnp.minimum(slots, CAP - 1))
    parity = (iota((8, 128), 0) & 1) == 0
    row_pair = lax.shift_right_logical(iota((1024, 128), 0), 1)
    lo_iota = iota((128, 128), 0)
    sub = iota((8, 128), 0)
    mine_ref[...] = jnp.full((8, 128), -1, jnp.int32)
    load.wait()
    for k in range(CAP):
        loads[k].wait()
        vox = jnp.max(jnp.where(sub == (jnp.maximum(found[k], 0) & 7), near_rows[k], -1), axis=0, keepdims=True)
        vox = jnp.where(found[k] >= 0, vox, -1)
        mine_ref[k : k + 1, :] = vox
        hi = lax.shift_right_arithmetic(vox, 7)
        onehot = (lo_iota == (vox & 127)).astype(F32).astype(BF16)
        wide = jnp.dot(table[...], onehot, preferred_element_type=F32)
        kept = jnp.where(row_pair == hi, wide, 0.0)
        kept = jnp.sum(kept.reshape(128, 8, 128), axis=0)
        re = jnp.sum(jnp.where(parity, kept, 0.0), axis=0, keepdims=True)
        im = jnp.sum(jnp.where(parity, 0.0, kept), axis=0, keepdims=True)
        for copy in range(8):
            stage[copy * 12 + 2 * k : copy * 12 + 2 * k + 1, :] = re
            stage[copy * 12 + 2 * k + 1 : copy * 12 + 2 * k + 2, :] = im
    block = stage[...].astype(BF16)
    for copy in range(8):
        out_ref[copy * 96 : (copy + 1) * 96, :] = block


def image_kernel(defocus_ref, part_ref, img_ref, sq_ref, wide):
    fy = (iota((KY, KX), 0) - KY // 2).astype(F32)
    fx = iota((KY, KX), 1).astype(F32)
    radius = (fy * fy + fx * fx) / float(BOX * BOX)
    phase0 = math.asin(AMP)
    pi_a = 3.140625
    pi_b = 9.67502593994140625e-4
    pi_c = math.pi - pi_a - pi_b
    coef = [(-1.0) ** k / math.factorial(2 * k + 1) for k in range(7)]
    for p in range(PER):
        wide[...] = part_ref[p * 512 : (p + 1) * 512, :].astype(F32)
        chi = (math.pi * WAVE * defocus_ref[p]) * radius
        whole = jnp.floor(chi * (1.0 / math.pi) + (phase0 / math.pi + 0.5))
        frac = ((chi - whole * pi_a) - whole * pi_b) - (whole * pi_c - phase0)
        half = whole * 0.5
        frac = frac * (1.0 - 4.0 * (half - jnp.floor(half)))
        sq = frac * frac
        poly = jnp.full_like(sq, coef[6])
        for k in range(5, -1, -1):
            poly = poly * sq + coef[k]
        ctf = -(poly * frac)
        sq_ref[p * KY : (p + 1) * KY, :] = ctf * ctf
        img_ref[p * 512 : p * 512 + KY, :] = ctf * wide[pl.ds(0, KY, stride=2), :]
        img_ref[p * 512 + KY : (p + 1) * 512, :] = ctf * wide[pl.ds(1, KY, stride=2), :]


CH = 64


def search_kernel(pos_ref, noise_ref, near_ref, far_ref, img_ref, sq_ref, fwd_ref, bwd_ref, corr_ref, back_ref,
                  sum_ref, far_out_ref, slots, rows_a, rows_b, q_a, q_b, power, corr, weight):
    slots[0 : 2 * HALF, :] = near_ref[...].astype(F32)
    slots[2 * HALF : 4 * HALF, :] = far_ref[...].astype(F32)

    def fetch(r, rows, k):
        for y in range(k * CH, (k + 1) * CH):
            at = pl.multiple_of(pos_ref[r, y], 2)
            rows[2 * y : 2 * y + 2, :] = slots[pl.ds(at, 2), :]

    def put(r, rows, k):
        for y in range(k * CH, (k + 1) * CH):
            at = pl.multiple_of(pos_ref[r, y], 2)
            sum_ref[pl.ds(at, 2), :] = rows[2 * y : 2 * y + 2, :]

    def images(p, k):
        at = p * 512 + k * CH
        return img_ref[at : at + CH, :], img_ref[at + KY : at + KY + CH, :]

    def score_ref(r, rows, q, ahead, ahead_rows):
        sums = [jnp.zeros((8, KX), F32) for _ in range(PER)]
        for k in range(KY // CH):
            fetch(ahead, ahead_rows, k)
            re = rows[pl.ds(2 * CH * k, CH, stride=2), :]
            im = rows[pl.ds(2 * CH * k + 1, CH, stride=2), :]
            mag = re * re + im * im
            for p in range(PER):
                a_re, a_im = images(p, k)
                q[k * CH : (k + 1) * CH, p * 256 : p * 256 + 128] = (re * a_re + im * a_im).astype(BF16)
                q[k * CH : (k + 1) * CH, p * 256 + 128 : (p + 1) * 256] = (re * a_im - im * a_re).astype(BF16)
                part = sq_ref[p * KY + k * CH : p * KY + (k + 1) * CH, :] * mag
                sums[p] = sums[p] + jnp.sum(part.reshape(CH // 8, 8, KX), axis=0)
        for p in range(PER):
            power[pl.ds(p * REFS + r, 1), :] = jnp.sum(sums[p], axis=0, keepdims=True)
        row_phase = jnp.dot(q[...], fwd_ref[...], preferred_element_type=F32).astype(BF16)
        both = jnp.dot(corr_ref[...], row_phase, preferred_element_type=F32)
        corr[pl.ds(pl.multiple_of(r * SHIFTS, SHIFTS), SHIFTS), :] = both[:SHIFTS, :128] - both[SHIFTS:, 128:]

    def forward(t, carry):
        r = 2 * t
        score_ref(r, rows_a, q_a, r + 1, rows_b)
        score_ref(r + 1, rows_b, q_b, jnp.minimum(r + 2, REFS - 1), rows_a)
        return carry

    for k in range(KY // CH):
        fetch(0, rows_a, k)
    lax.fori_loop(0, REFS // 2, forward, 0)

    group = lax.shift_right_logical(iota((1, 128), 1), 5)
    noise = jnp.zeros((1, 128), F32)
    totals = jnp.zeros((REFS, 128), F32)
    for p in range(PER):
        noise = jnp.where(group == p, noise_ref[p], noise)
        column = jnp.sum(power[p * REFS : (p + 1) * REFS, :], axis=1, keepdims=True)
        totals = jnp.where(group == p, column, totals)
    score = corr[...].reshape(REFS, SHIFTS, 128) - 0.5 * totals[:, None, :]
    score = score.reshape(REFS * SHIFTS, 128) * noise
    top = jnp.max(score, axis=0, keepdims=True)
    peak = jnp.zeros((1, 128), F32)
    for p in range(PER):
        peak = jnp.where(group == p, jnp.max(jnp.where(group == p, top, -jnp.inf), axis=1, keepdims=True), peak)
    expo = jnp.exp(score - peak)
    lane_sum = jnp.sum(expo, axis=0, keepdims=True)
    norm = jnp.ones((1, 128), F32)
    for p in range(PER):
        norm = jnp.where(group == p, jnp.sum(jnp.where(group == p, lane_sum, 0.0), axis=1, keepdims=True), norm)
    weight[...] = (expo * (1.0 / norm)).astype(BF16)
    sum_ref[...] = jnp.zeros_like(sum_ref)

    def insert_ref(r, rows, behind, behind_rows):
        w = weight[pl.ds(pl.multiple_of(r * SHIFTS, SHIFTS), SHIFTS), :]
        col = jnp.dot(back_ref[...], w, preferred_element_type=F32).astype(BF16)
        col = jnp.concatenate([col[:KY], col[KY:]], axis=1)
        for k in range(KY // CH):
            put(behind, behind_rows, k)
            ss = jnp.dot(col[k * CH : (k + 1) * CH], bwd_ref[...], preferred_element_type=F32).astype(BF16).astype(F32)
            t_re = t_im = None
            for p in range(PER):
                a_re, a_im = images(p, k)
                s_re = ss[:, p * 256 : p * 256 + 128]
                s_im = ss[:, p * 256 + 128 : (p + 1) * 256]
                u_re = a_re * s_re - a_im * s_im
                u_im = a_re * s_im + a_im * s_re
                t_re = u_re if t_re is None else t_re + u_re
                t_im = u_im if t_im is None else t_im + u_im
            rows[pl.ds(2 * CH * k, CH, stride=2), :] = t_re
            rows[pl.ds(2 * CH * k + 1, CH, stride=2), :] = t_im

    def backward(t, carry):
        r = 2 * t
        insert_ref(r, rows_a, (r + REFS - 1) % REFS, rows_b)
        insert_ref(r + 1, rows_b, r, rows_a)
        return carry

    lax.fori_loop(0, REFS // 2, backward, 0)
    for k in range(KY // CH):
        put(REFS - 1, rows_b, k)
    far_out_ref[...] = sum_ref[2 * HALF : 4 * HALF, :].astype(BF16)


def insert_kernel(mine_ref, got_ref, out_ref, wide, left, right):
    sums = jnp.sum(got_ref[...].astype(F32).reshape(32, 24, 128), axis=0)
    wide[...] = sums * (1.0 / math.sqrt(PARTICLES))
    hi_iota = iota((512, 128), 0)
    lo_iota = iota((128, 128), 0)
    for k in range(CAP):
        vox = mine_ref[k : k + 1, :]
        hi = lax.shift_right_arithmetic(vox, 7)
        onehot = (lo_iota == (vox & 127)).astype(F32).astype(BF16)
        right[:, 2 * k * 128 : (2 * k + 1) * 128] = onehot
        right[:, (2 * k + 1) * 128 : (2 * k + 2) * 128] = onehot
        at = hi_iota == hi
        for c in range(2):
            total = wide[2 * k + c : 2 * k + c + 1, :] + wide[12 + 2 * k + c : 12 + 2 * k + c + 1, :]
            first = total.astype(BF16).astype(F32)
            rest = total - first
            left[c, :, 2 * k * 128 : (2 * k + 1) * 128] = jnp.where(at, first, 0.0).astype(BF16)
            left[c, :, (2 * k + 1) * 128 : (2 * k + 2) * 128] = jnp.where(at, rest, 0.0).astype(BF16)
    for c in range(2):
        out_ref[pl.ds(c, 512, stride=2), :] = lax.dot_general(
            left[c], right[...], (((1,), (1,)), ((), ())), preferred_element_type=F32
        )


VM = pl.BlockSpec(memory_space=pltpu.VMEM)
SM = pl.BlockSpec(memory_space=pltpu.SMEM)
ANY = pl.BlockSpec(memory_space=pl.ANY)


def shape(dims, dtype):
    return jax.ShapeDtypeStruct(dims, dtype)


def params():
    return pltpu.CompilerParams(vmem_limit_bytes=VMEM_LIMIT)


def cost(us):
    return pl.CostEstimate(flops=int(us * 1e9), bytes_accessed=int(us * 1e6), transcendentals=0)


def pick_call(me, owner, volume_rows, voxel_rows):
    return pl.pallas_call(
        pick_kernel,
        out_shape=(
            shape((REFS, KY), jnp.int32),
            shape((8, 128), jnp.int32),
            shape((64 * 12, 128), BF16),
        ),
        in_specs=[SM, VM, ANY, ANY],
        out_specs=(VM, VM, VM),
        scratch_shapes=[
            pltpu.VMEM((REFS, KY), jnp.int32),
            pltpu.VMEM((96, 128), F32),
            pltpu.VMEM((1024, 128), BF16),
            pltpu.VMEM((CAP, 8, 128), jnp.int32),
            pltpu.SemaphoreType.DMA((CAP + 1,)),
        ],
        compiler_params=pltpu.CompilerParams(vmem_limit_bytes=60 * 1024 * 1024),
        name="pick_rows",
    )(me, owner, volume_rows, voxel_rows)


def image_call(defocus, particle_rows):
    return pl.pallas_call(
        image_kernel,
        out_shape=(shape((PER * 512, KX), F32), shape((PER * KY, KX), F32)),
        in_specs=[SM, VM],
        out_specs=(VM, VM),
        scratch_shapes=[pltpu.VMEM((512, KX), F32)],
        compiler_params=params(),
        cost_estimate=cost(4),
        name="ctf_images",
    )(defocus, particle_rows)


def search_call(pos, noise, near, far, img, sq):
    tables = [jnp.asarray(t) for t in phase_constants()]
    return pl.pallas_call(
        search_kernel,
        out_shape=(shape((4 * HALF, KX), F32), shape((2 * HALF, KX), BF16)),
        in_specs=[SM, SM] + [VM] * 8,
        out_specs=(VM, VM),
        scratch_shapes=[
            pltpu.VMEM((4 * HALF, KX), F32),
            pltpu.VMEM((2 * KY, KX), F32),
            pltpu.VMEM((2 * KY, KX), F32),
            pltpu.VMEM((KY, PER * 2 * KX), BF16),
            pltpu.VMEM((KY, PER * 2 * KX), BF16),
            pltpu.VMEM((PER * REFS, KX), F32),
            pltpu.VMEM((REFS * SHIFTS, 128), F32),
            pltpu.VMEM((REFS * SHIFTS, 128), BF16),
        ],
        compiler_params=params(),
        name="shift_search",
    )(pos, noise, near, far, img, sq, *tables)


def insert_call(mine, got):
    return pl.pallas_call(
        insert_kernel,
        out_shape=shape((1024, 128), F32),
        in_specs=[VM, VM],
        out_specs=VM,
        scratch_shapes=[
            pltpu.VMEM((24, 128), F32),
            pltpu.VMEM((2, 512, 2 * CAP * 128), BF16),
            pltpu.VMEM((128, 2 * CAP * 128), BF16),
        ],
        compiler_params=params(),
        name="insert_rows",
    )(mine, got)


def local(particles, defocus, inverse_noise, volume, slice_owner, slice_voxel):
    me = lax.axis_index(FINE).astype(jnp.int32).reshape(1)
    volume_rows = volume.reshape(2, 512, 128).transpose(1, 0, 2).reshape(1024, 128)
    pos, mine, compact = pick_call(me, slice_owner, volume_rows, slice_voxel.reshape(ROWS, KX))
    line = lax.all_to_all(compact.reshape(64, CAP, 2, 128), ("zh", "zl", "y"), 0, 0, tiled=True)
    spread = jnp.broadcast_to(line.reshape(1, 384, 2, 128), (4, 384, 2, 128))
    near = lax.all_to_all(spread, "x", 0, 0, tiled=True).reshape(HALF, 2, 128)
    swap = [(0, 1), (1, 0)]
    far = lax.ppermute(near, "c", swap)
    img, sq = image_call(defocus, particles.reshape(PER * KY * 2, KX))
    sums, far_out = search_call(
        pos, inverse_noise, near.reshape(2 * HALF, 128), far.reshape(2 * HALF, 128), img, sq
    )
    received = lax.ppermute(far_out.reshape(HALF, 2, 128), "c", swap)
    pair = sums[: 2 * HALF].reshape(HALF, 2, 128) + received.astype(F32)
    plane = lax.all_to_all(pair.astype(BF16).reshape(4, 384, 2, 128), "x", 0, 0, tiled=True)
    plane = jnp.sum(plane.astype(F32), axis=0).astype(BF16)
    last = lax.all_to_all(plane.reshape(64, CAP, 2, 128), ("zh", "zl", "y"), 0, 0, tiled=True)
    out = insert_call(mine, last.reshape(768, 128))
    return out.reshape(512, 2, 128).transpose(1, 0, 2).reshape(2, 65536)


def solution(mesh):
    fine = Mesh(mesh.devices.reshape(4, 2, 8, 4, 2), FINE)
    in_specs = (P(FINE, None, None, None), P(FINE), P(FINE), P(None, FINE), P(), P())
    return jax.shard_map(local, mesh=fine, in_specs=in_specs, out_specs=P(None, FINE), check_vma=False)
```

```python
import math

import jax
import jax.numpy as jnp
import ml_dtypes
import numpy as np
from jax import lax
from jax.experimental import pallas as pl
from jax.experimental.pallas import tpu as pltpu
from jax.sharding import Mesh
from jax.sharding import PartitionSpec as P

KY, KX, REFS, SHIFTS, CAP, PER = 256, 128, 8, 32, 6, 4
ROWS = REFS * KY
PARTICLES = 2048
HALF = 1536
BOX = 400
WAVE = 0.0197
AMP = 0.1
VMEM_LIMIT = 40 * 1024 * 1024
FINE = ("zh", "c", "y", "x", "zl")
F32 = jnp.float32
BF16 = jnp.bfloat16


def phase_constants():
    shift = np.arange(SHIFTS) - SHIFTS // 2
    fy = np.arange(KY) - KY // 2
    fx = np.arange(KX)
    ang_y = 2.0 * np.pi / BOX * np.mod(fy[:, None] * shift[None, :], BOX)
    ang_x = 2.0 * np.pi / BOX * np.mod(fx[:, None] * shift[None, :], BOX)
    cos_y, sin_y, cos_x, sin_x = np.cos(ang_y), np.sin(ang_y), np.cos(ang_x), np.sin(ang_x)
    fwd = np.zeros((PER, 2, KX, 2, PER, SHIFTS))
    bwd = np.zeros((2, PER, SHIFTS, PER, 2, KX))
    for p in range(PER):
        fwd[p, 0, :, 0, p], fwd[p, 0, :, 1, p] = cos_x, sin_x
        fwd[p, 1, :, 0, p], fwd[p, 1, :, 1, p] = -sin_x, cos_x
        bwd[0, p, :, p, 0], bwd[0, p, :, p, 1] = cos_x.T, sin_x.T
        bwd[1, p, :, p, 0], bwd[1, p, :, p, 1] = -sin_x.T, cos_x.T
    fwd = fwd.reshape(PER * 2 * KX, 2 * PER * SHIFTS)
    bwd = bwd.reshape(2 * PER * SHIFTS, PER * 2 * KX)
    corr = np.concatenate([cos_y.T, sin_y.T], axis=0)
    back = np.concatenate([cos_y, sin_y], axis=0)
    return [a.astype(np.float32).astype(ml_dtypes.bfloat16) for a in (fwd, bwd, corr, back)]


def iota(shape, dim):
    return lax.broadcasted_iota(jnp.int32, shape, dim)


def pick_kernel(me_ref, own_hbm, vol_hbm, vox_hbm, pos_ref, mine_ref, out_ref, owners, slot, stage, table, voxels, sems):
    load_own = pltpu.make_async_copy(own_hbm, owners, sems.at[0])
    load_vox = pltpu.make_async_copy(vox_hbm, voxels, sems.at[1])
    load_vol = pltpu.make_async_copy(vol_hbm, table, sems.at[2])
    load_own.start()
    load_vox.start()
    load_vol.start()
    me = me_ref[0]
    load_own.wait()
    own = owners[...]
    turned = own.astype(F32).T
    cols, here = [], []
    for b in range(ROWS // 128):
        r, h = b // 2, b % 2
        cols.append(jnp.broadcast_to(turned[h * 128 : (h + 1) * 128, r : r + 1], (128, 128)))
        here.append(jnp.broadcast_to(own[r : r + 1, h * 128 : (h + 1) * 128].astype(F32), (128, 128)))
    earlier = iota((128, 128), 0) < iota((128, 128), 1)
    for b in range(ROWS // 128):
        r, h = b // 2, b % 2
        hits = ((cols[b] == here[b]) & earlier).astype(F32)
        for c in range(b):
            hits = hits + (cols[c] == here[b]).astype(F32)
        slot[r : r + 1, h * 128 : (h + 1) * 128] = jnp.sum(hits, axis=0, keepdims=True).astype(jnp.int32)
    slots = slot[...]
    row_id = iota((REFS, KY), 0) * KY + iota((REFS, KY), 1)
    is_me = own == me
    found = [jnp.max(jnp.where(is_me & (slots == k), row_id, -1)) for k in range(CAP)]
    z = lax.shift_right_logical(own, 7) * 2 + (own & 1)
    y = lax.shift_right_logical(own, 3) & 7
    x = lax.shift_right_logical(own, 1) & 3
    across = ((lax.shift_right_logical(own, 6) ^ lax.shift_right_logical(me, 6)) & 1) * HALF
    pos_ref[...] = 2 * (across + x * (64 * CAP) + (z * 8 + y) * CAP + jnp.minimum(slots, CAP - 1))
    parity = (iota((8, 128), 0) & 1) == 0
    row_pair = lax.shift_right_logical(iota((1024, 128), 0), 1)
    lo_iota = iota((128, 128), 0)
    mine_ref[...] = jnp.full((8, 128), -1, jnp.int32)
    load_vox.wait()
    load_vol.wait()
    for k in range(CAP):
        vox = voxels[pl.ds(jnp.maximum(found[k], 0), 1), :]
        vox = jnp.where(found[k] >= 0, vox, -1)
        mine_ref[k : k + 1, :] = vox
        hi = lax.shift_right_arithmetic(vox, 7)
        onehot = (lo_iota == (vox & 127)).astype(F32).astype(BF16)
        wide = jnp.dot(table[...], onehot, preferred_element_type=F32)
        kept = jnp.where(row_pair == hi, wide, 0.0)
        kept = jnp.sum(kept.reshape(128, 8, 128), axis=0)
        re = jnp.sum(jnp.where(parity, kept, 0.0), axis=0, keepdims=True)
        im = jnp.sum(jnp.where(parity, 0.0, kept), axis=0, keepdims=True)
        for copy in range(8):
            stage[copy * 12 + 2 * k : copy * 12 + 2 * k + 1, :] = re
            stage[copy * 12 + 2 * k + 1 : copy * 12 + 2 * k + 2, :] = im
    block = stage[...].astype(BF16)
    for copy in range(8):
        out_ref[copy * 96 : (copy + 1) * 96, :] = block


def image_kernel(defocus_ref, part_ref, img_ref, sq_ref, wide):
    fy = (iota((KY, KX), 0) - KY // 2).astype(F32)
    fx = iota((KY, KX), 1).astype(F32)
    radius = (fy * fy + fx * fx) / float(BOX * BOX)
    phase0 = math.asin(AMP)
    pi_a = 3.140625
    pi_b = 9.67502593994140625e-4
    pi_c = math.pi - pi_a - pi_b
    coef = [(-1.0) ** k / math.factorial(2 * k + 1) for k in range(7)]
    for p in range(PER):
        wide[...] = part_ref[p * 512 : (p + 1) * 512, :].astype(F32)
        chi = (math.pi * WAVE * defocus_ref[p]) * radius
        whole = jnp.floor(chi * (1.0 / math.pi) + (phase0 / math.pi + 0.5))
        frac = ((chi - whole * pi_a) - whole * pi_b) - (whole * pi_c - phase0)
        half = whole * 0.5
        frac = frac * (1.0 - 4.0 * (half - jnp.floor(half)))
        sq = frac * frac
        poly = jnp.full_like(sq, coef[6])
        for k in range(5, -1, -1):
            poly = poly * sq + coef[k]
        ctf = -(poly * frac)
        sq_ref[p * KY : (p + 1) * KY, :] = ctf * ctf
        img_ref[p * 512 : p * 512 + KY, :] = ctf * wide[pl.ds(0, KY, stride=2), :]
        img_ref[p * 512 + KY : (p + 1) * 512, :] = ctf * wide[pl.ds(1, KY, stride=2), :]


CH = 64


def search_kernel(pos_ref, noise_ref, near_ref, far_ref, img_ref, sq_ref, fwd_ref, bwd_ref, corr_ref, back_ref,
                  sum_ref, far_out_ref, slots, rows_a, rows_b, q_a, q_b, power, corr, weight):
    slots[0 : 2 * HALF, :] = near_ref[...].astype(F32)
    slots[2 * HALF : 4 * HALF, :] = far_ref[...].astype(F32)

    def fetch(r, rows, k):
        for y in range(k * CH, (k + 1) * CH):
            at = pl.multiple_of(pos_ref[r, y], 2)
            rows[2 * y : 2 * y + 2, :] = slots[pl.ds(at, 2), :]

    def put(r, rows, k):
        for y in range(k * CH, (k + 1) * CH):
            at = pl.multiple_of(pos_ref[r, y], 2)
            sum_ref[pl.ds(at, 2), :] = rows[2 * y : 2 * y + 2, :]

    def images(p, k):
        at = p * 512 + k * CH
        return img_ref[at : at + CH, :], img_ref[at + KY : at + KY + CH, :]

    def score_ref(r, rows, q, ahead, ahead_rows):
        sums = [jnp.zeros((8, KX), F32) for _ in range(PER)]
        for k in range(KY // CH):
            fetch(ahead, ahead_rows, k)
            re = rows[pl.ds(2 * CH * k, CH, stride=2), :]
            im = rows[pl.ds(2 * CH * k + 1, CH, stride=2), :]
            mag = re * re + im * im
            for p in range(PER):
                a_re, a_im = images(p, k)
                q[k * CH : (k + 1) * CH, p * 256 : p * 256 + 128] = (re * a_re + im * a_im).astype(BF16)
                q[k * CH : (k + 1) * CH, p * 256 + 128 : (p + 1) * 256] = (re * a_im - im * a_re).astype(BF16)
                part = sq_ref[p * KY + k * CH : p * KY + (k + 1) * CH, :] * mag
                sums[p] = sums[p] + jnp.sum(part.reshape(CH // 8, 8, KX), axis=0)
        for p in range(PER):
            power[pl.ds(p * REFS + r, 1), :] = jnp.sum(sums[p], axis=0, keepdims=True)
        row_phase = jnp.dot(q[...], fwd_ref[...], preferred_element_type=F32).astype(BF16)
        both = jnp.dot(corr_ref[...], row_phase, preferred_element_type=F32)
        corr[pl.ds(pl.multiple_of(r * SHIFTS, SHIFTS), SHIFTS), :] = both[:SHIFTS, :128] - both[SHIFTS:, 128:]

    def forward(t, carry):
        r = 2 * t
        score_ref(r, rows_a, q_a, r + 1, rows_b)
        score_ref(r + 1, rows_b, q_b, jnp.minimum(r + 2, REFS - 1), rows_a)
        return carry

    for k in range(KY // CH):
        fetch(0, rows_a, k)
    lax.fori_loop(0, REFS // 2, forward, 0)

    group = lax.shift_right_logical(iota((1, 128), 1), 5)
    noise = jnp.zeros((1, 128), F32)
    totals = jnp.zeros((REFS, 128), F32)
    for p in range(PER):
        noise = jnp.where(group == p, noise_ref[p], noise)
        column = jnp.sum(power[p * REFS : (p + 1) * REFS, :], axis=1, keepdims=True)
        totals = jnp.where(group == p, column, totals)
    score = corr[...].reshape(REFS, SHIFTS, 128) - 0.5 * totals[:, None, :]
    score = score.reshape(REFS * SHIFTS, 128) * noise
    top = jnp.max(score, axis=0, keepdims=True)
    peak = jnp.zeros((1, 128), F32)
    for p in range(PER):
        peak = jnp.where(group == p, jnp.max(jnp.where(group == p, top, -jnp.inf), axis=1, keepdims=True), peak)
    expo = jnp.exp(score - peak)
    lane_sum = jnp.sum(expo, axis=0, keepdims=True)
    norm = jnp.ones((1, 128), F32)
    for p in range(PER):
        norm = jnp.where(group == p, jnp.sum(jnp.where(group == p, lane_sum, 0.0), axis=1, keepdims=True), norm)
    weight[...] = (expo * (1.0 / norm)).astype(BF16)
    sum_ref[...] = jnp.zeros_like(sum_ref)

    def insert_ref(r, rows, behind, behind_rows):
        w = weight[pl.ds(pl.multiple_of(r * SHIFTS, SHIFTS), SHIFTS), :]
        col = jnp.dot(back_ref[...], w, preferred_element_type=F32).astype(BF16)
        col = jnp.concatenate([col[:KY], col[KY:]], axis=1)
        shifted = jnp.dot(col, bwd_ref[...], preferred_element_type=F32).astype(BF16)
        for k in range(KY // CH):
            put(behind, behind_rows, k)
            ss = shifted[k * CH : (k + 1) * CH].astype(F32)
            t_re = t_im = None
            for p in range(PER):
                a_re, a_im = images(p, k)
                s_re = ss[:, p * 256 : p * 256 + 128]
                s_im = ss[:, p * 256 + 128 : (p + 1) * 256]
                u_re = a_re * s_re - a_im * s_im
                u_im = a_re * s_im + a_im * s_re
                t_re = u_re if t_re is None else t_re + u_re
                t_im = u_im if t_im is None else t_im + u_im
            rows[pl.ds(2 * CH * k, CH, stride=2), :] = t_re
            rows[pl.ds(2 * CH * k + 1, CH, stride=2), :] = t_im

    def backward(t, carry):
        r = 2 * t
        insert_ref(r, rows_a, (r + REFS - 1) % REFS, rows_b)
        insert_ref(r + 1, rows_b, r, rows_a)
        return carry

    lax.fori_loop(0, REFS // 2, backward, 0)
    for k in range(KY // CH):
        put(REFS - 1, rows_b, k)
    far_out_ref[...] = sum_ref[2 * HALF : 4 * HALF, :].astype(BF16)


def insert_kernel(mine_ref, got_ref, out_ref, wide, left, right):
    sums = jnp.sum(got_ref[...].astype(F32).reshape(32, 24, 128), axis=0)
    wide[...] = sums * (1.0 / math.sqrt(PARTICLES))
    hi_iota = iota((512, 128), 0)
    lo_iota = iota((128, 128), 0)
    for k in range(CAP):
        vox = mine_ref[k : k + 1, :]
        hi = lax.shift_right_arithmetic(vox, 7)
        onehot = (lo_iota == (vox & 127)).astype(F32).astype(BF16)
        right[:, 2 * k * 128 : (2 * k + 1) * 128] = onehot
        right[:, (2 * k + 1) * 128 : (2 * k + 2) * 128] = onehot
        at = hi_iota == hi
        for c in range(2):
            total = wide[2 * k + c : 2 * k + c + 1, :] + wide[12 + 2 * k + c : 12 + 2 * k + c + 1, :]
            first = total.astype(BF16).astype(F32)
            rest = total - first
            left[c, :, 2 * k * 128 : (2 * k + 1) * 128] = jnp.where(at, first, 0.0).astype(BF16)
            left[c, :, (2 * k + 1) * 128 : (2 * k + 2) * 128] = jnp.where(at, rest, 0.0).astype(BF16)
    for c in range(2):
        out_ref[pl.ds(c, 512, stride=2), :] = lax.dot_general(
            left[c], right[...], (((1,), (1,)), ((), ())), preferred_element_type=F32
        )


def pair_kernel(sums_ref, got_ref, out_ref):
    out_ref[...] = (sums_ref[0 : 2 * HALF, :] + got_ref[...].astype(F32)).astype(BF16)


def line_kernel(got_ref, out_ref):
    total = got_ref[0:768, :].astype(F32)
    for k in range(1, 4):
        total = total + got_ref[k * 768 : (k + 1) * 768, :].astype(F32)
    out_ref[...] = total.astype(BF16)


VM = pl.BlockSpec(memory_space=pltpu.VMEM)
SM = pl.BlockSpec(memory_space=pltpu.SMEM)
ANY = pl.BlockSpec(memory_space=pl.ANY)


def shape(dims, dtype):
    return jax.ShapeDtypeStruct(dims, dtype)


def params():
    return pltpu.CompilerParams(vmem_limit_bytes=VMEM_LIMIT)


def cost(us):
    return pl.CostEstimate(flops=int(us * 1e9), bytes_accessed=int(us * 1e6), transcendentals=0)


def pick_call(me, owner, volume_rows, voxel_rows):
    return pl.pallas_call(
        pick_kernel,
        out_shape=(
            shape((REFS, KY), jnp.int32),
            shape((8, 128), jnp.int32),
            shape((64 * 12, 128), BF16),
        ),
        in_specs=[SM, ANY, ANY, ANY],
        out_specs=(VM, VM, VM),
        scratch_shapes=[
            pltpu.VMEM((REFS, KY), jnp.int32),
            pltpu.VMEM((REFS, KY), jnp.int32),
            pltpu.VMEM((96, 128), F32),
            pltpu.VMEM((1024, 128), BF16),
            pltpu.VMEM((ROWS, KX), jnp.int32),
            pltpu.SemaphoreType.DMA((3,)),
        ],
        compiler_params=pltpu.CompilerParams(vmem_limit_bytes=60 * 1024 * 1024),
        name="pick_rows",
    )(me, owner, volume_rows, voxel_rows)


def image_call(defocus, particle_rows):
    return pl.pallas_call(
        image_kernel,
        out_shape=(shape((PER * 512, KX), F32), shape((PER * KY, KX), F32)),
        in_specs=[SM, VM],
        out_specs=(VM, VM),
        scratch_shapes=[pltpu.VMEM((512, KX), F32)],
        compiler_params=params(),
        cost_estimate=cost(4),
        name="ctf_images",
    )(defocus, particle_rows)


def search_call(pos, noise, near, far, img, sq):
    tables = [jnp.asarray(t) for t in phase_constants()]
    return pl.pallas_call(
        search_kernel,
        out_shape=(shape((4 * HALF, KX), F32), shape((2 * HALF, KX), BF16)),
        in_specs=[SM, SM] + [VM] * 8,
        out_specs=(VM, VM),
        scratch_shapes=[
            pltpu.VMEM((4 * HALF, KX), F32),
            pltpu.VMEM((2 * KY, KX), F32),
            pltpu.VMEM((2 * KY, KX), F32),
            pltpu.VMEM((KY, PER * 2 * KX), BF16),
            pltpu.VMEM((KY, PER * 2 * KX), BF16),
            pltpu.VMEM((PER * REFS, KX), F32),
            pltpu.VMEM((REFS * SHIFTS, 128), F32),
            pltpu.VMEM((REFS * SHIFTS, 128), BF16),
        ],
        compiler_params=params(),
        name="shift_search",
    )(pos, noise, near, far, img, sq, *tables)


def small_call(kernel, name, rows, *args):
    return pl.pallas_call(
        kernel,
        out_shape=shape((rows, 128), BF16),
        in_specs=[VM] * len(args),
        out_specs=VM,
        compiler_params=params(),
        name=name,
    )(*args)


def insert_call(mine, got):
    return pl.pallas_call(
        insert_kernel,
        out_shape=shape((1024, 128), F32),
        in_specs=[VM, VM],
        out_specs=VM,
        scratch_shapes=[
            pltpu.VMEM((24, 128), F32),
            pltpu.VMEM((2, 512, 2 * CAP * 128), BF16),
            pltpu.VMEM((128, 2 * CAP * 128), BF16),
        ],
        compiler_params=params(),
        name="insert_rows",
    )(mine, got)


def local(particles, defocus, inverse_noise, volume, slice_owner, slice_voxel):
    me = lax.axis_index(FINE).astype(jnp.int32).reshape(1)
    volume_rows = volume.reshape(2, 512, 128).transpose(1, 0, 2).reshape(1024, 128)
    pos, mine, compact = pick_call(me, slice_owner, volume_rows, slice_voxel.reshape(ROWS, KX))
    line = lax.all_to_all(compact.reshape(64, CAP, 2, 128), ("zh", "zl", "y"), 0, 0, tiled=True)
    spread = jnp.broadcast_to(line.reshape(1, 384, 2, 128), (4, 384, 2, 128))
    near = lax.all_to_all(spread, "x", 0, 0, tiled=True).reshape(HALF, 2, 128)
    swap = [(0, 1), (1, 0)]
    far = lax.ppermute(near, "c", swap)
    img, sq = image_call(defocus, particles.reshape(PER * KY * 2, KX))
    sums, far_out = search_call(
        pos, inverse_noise, near.reshape(2 * HALF, 128), far.reshape(2 * HALF, 128), img, sq
    )
    received = lax.ppermute(far_out.reshape(HALF, 2, 128), "c", swap)
    pair = small_call(pair_kernel, "add_core", 2 * HALF, sums, received.reshape(2 * HALF, 128))
    plane = lax.all_to_all(pair.reshape(4, 384, 2, 128), "x", 0, 0, tiled=True)
    plane = small_call(line_kernel, "add_line", 768, plane.reshape(2 * HALF, 128))
    last = lax.all_to_all(plane.reshape(64, CAP, 2, 128), ("zh", "zl", "y"), 0, 0, tiled=True)
    out = insert_call(mine, last.reshape(768, 128))
    return out.reshape(512, 2, 128).transpose(1, 0, 2).reshape(2, 65536)


def solution(mesh):
    fine = Mesh(mesh.devices.reshape(4, 2, 8, 4, 2), FINE)
    in_specs = (P(FINE, None, None, None), P(FINE), P(FINE), P(None, FINE), P(), P())
    return jax.shard_map(local, mesh=fine, in_specs=in_specs, out_specs=P(None, FINE), check_vma=False)
```

```python
import math

import jax
import jax.numpy as jnp
import ml_dtypes
import numpy as np
from jax import lax
from jax.experimental import pallas as pl
from jax.experimental.pallas import tpu as pltpu
from jax.sharding import Mesh
from jax.sharding import PartitionSpec as P

KY, KX, REFS, SHIFTS, CAP, PER = 256, 128, 8, 32, 6, 4
ROWS = REFS * KY
PARTICLES = 2048
HALF = 1536
BOX = 400
WAVE = 0.0197
AMP = 0.1
VMEM_LIMIT = 40 * 1024 * 1024
FINE = ("zh", "c", "y", "x", "zl")
F32 = jnp.float32
BF16 = jnp.bfloat16


def phase_constants():
    shift = np.arange(SHIFTS) - SHIFTS // 2
    fy = np.arange(KY) - KY // 2
    fx = np.arange(KX)
    ang_y = 2.0 * np.pi / BOX * np.mod(fy[:, None] * shift[None, :], BOX)
    ang_x = 2.0 * np.pi / BOX * np.mod(fx[:, None] * shift[None, :], BOX)
    cos_y, sin_y, cos_x, sin_x = np.cos(ang_y), np.sin(ang_y), np.cos(ang_x), np.sin(ang_x)
    fwd = np.zeros((PER, 2, KX, 2, PER, SHIFTS))
    bwd = np.zeros((2, PER, SHIFTS, PER, 2, KX))
    for p in range(PER):
        fwd[p, 0, :, 0, p], fwd[p, 0, :, 1, p] = cos_x, sin_x
        fwd[p, 1, :, 0, p], fwd[p, 1, :, 1, p] = -sin_x, cos_x
        bwd[0, p, :, p, 0], bwd[0, p, :, p, 1] = cos_x.T, sin_x.T
        bwd[1, p, :, p, 0], bwd[1, p, :, p, 1] = -sin_x.T, cos_x.T
    fwd = fwd.reshape(PER * 2 * KX, 2 * PER * SHIFTS)
    bwd = bwd.reshape(2 * PER * SHIFTS, PER * 2 * KX)
    corr = np.concatenate([cos_y.T, sin_y.T], axis=0)
    back = np.concatenate([cos_y, sin_y], axis=0)
    return [a.astype(np.float32).astype(ml_dtypes.bfloat16) for a in (fwd, bwd, corr, back)]


def iota(shape, dim):
    return lax.broadcasted_iota(jnp.int32, shape, dim)


def pick_kernel(me_ref, own_hbm, vol_hbm, vox_hbm, pos_ref, mine_ref, out_ref, owners, slot, stage, table, voxels, sems):
    load_own = pltpu.make_async_copy(own_hbm, owners, sems.at[0])
    load_vox = pltpu.make_async_copy(vox_hbm, voxels, sems.at[1])
    load_vol = pltpu.make_async_copy(vol_hbm, table, sems.at[2])
    load_own.start()
    load_vox.start()
    load_vol.start()
    me = me_ref[0]
    load_own.wait()
    own = owners[...]
    turned = own.astype(F32).T
    cols, here = [], []
    for b in range(ROWS // 128):
        r, h = b // 2, b % 2
        cols.append(jnp.broadcast_to(turned[h * 128 : (h + 1) * 128, r : r + 1], (128, 128)))
        here.append(jnp.broadcast_to(own[r : r + 1, h * 128 : (h + 1) * 128].astype(F32), (128, 128)))
    earlier = iota((128, 128), 0) < iota((128, 128), 1)
    for b in range(ROWS // 128):
        r, h = b // 2, b % 2
        hits = ((cols[b] == here[b]) & earlier).astype(F32)
        for c in range(b):
            hits = hits + (cols[c] == here[b]).astype(F32)
        slot[r : r + 1, h * 128 : (h + 1) * 128] = jnp.sum(hits, axis=0, keepdims=True).astype(jnp.int32)
    slots = slot[...]
    row_id = iota((REFS, KY), 0) * KY + iota((REFS, KY), 1)
    is_me = own == me
    found = [jnp.max(jnp.where(is_me & (slots == k), row_id, -1)) for k in range(CAP)]
    z = lax.shift_right_logical(own, 7) * 2 + (own & 1)
    y = lax.shift_right_logical(own, 3) & 7
    x = lax.shift_right_logical(own, 1) & 3
    across = ((lax.shift_right_logical(own, 6) ^ lax.shift_right_logical(me, 6)) & 1) * HALF
    pos_ref[...] = 2 * (across + x * (64 * CAP) + (z * 8 + y) * CAP + jnp.minimum(slots, CAP - 1))
    parity = (iota((8, 128), 0) & 1) == 0
    row_pair = lax.shift_right_logical(iota((1024, 128), 0), 1)
    lo_iota = iota((128, 128), 0)
    mine_ref[...] = jnp.full((8, 128), -1, jnp.int32)
    load_vox.wait()
    load_vol.wait()
    for k in range(CAP):
        vox = voxels[pl.ds(jnp.maximum(found[k], 0), 1), :]
        vox = jnp.where(found[k] >= 0, vox, -1)
        mine_ref[k : k + 1, :] = vox
        hi = lax.shift_right_arithmetic(vox, 7)
        onehot = (lo_iota == (vox & 127)).astype(F32).astype(BF16)
        wide = jnp.dot(table[...], onehot, preferred_element_type=F32)
        kept = jnp.where(row_pair == hi, wide, 0.0)
        kept = jnp.sum(kept.reshape(128, 8, 128), axis=0)
        re = jnp.sum(jnp.where(parity, kept, 0.0), axis=0, keepdims=True)
        im = jnp.sum(jnp.where(parity, 0.0, kept), axis=0, keepdims=True)
        for copy in range(8):
            stage[copy * 12 + 2 * k : copy * 12 + 2 * k + 1, :] = re
            stage[copy * 12 + 2 * k + 1 : copy * 12 + 2 * k + 2, :] = im
    block = stage[...].astype(BF16)
    for copy in range(8):
        out_ref[copy * 96 : (copy + 1) * 96, :] = block


def image_kernel(defocus_ref, part_ref, img_ref, sq_ref, wide):
    fy = (iota((KY, KX), 0) - KY // 2).astype(F32)
    fx = iota((KY, KX), 1).astype(F32)
    radius = (fy * fy + fx * fx) / float(BOX * BOX)
    phase0 = math.asin(AMP)
    pi_a = 3.140625
    pi_b = 9.67502593994140625e-4
    pi_c = math.pi - pi_a - pi_b
    coef = [(-1.0) ** k / math.factorial(2 * k + 1) for k in range(7)]
    for p in range(PER):
        wide[...] = part_ref[p * 512 : (p + 1) * 512, :].astype(F32)
        chi = (math.pi * WAVE * defocus_ref[p]) * radius
        whole = jnp.floor(chi * (1.0 / math.pi) + (phase0 / math.pi + 0.5))
        frac = ((chi - whole * pi_a) - whole * pi_b) - (whole * pi_c - phase0)
        half = whole * 0.5
        frac = frac * (1.0 - 4.0 * (half - jnp.floor(half)))
        sq = frac * frac
        poly = jnp.full_like(sq, coef[6])
        for k in range(5, -1, -1):
            poly = poly * sq + coef[k]
        ctf = -(poly * frac)
        sq_ref[p * KY : (p + 1) * KY, :] = ctf * ctf
        img_ref[p * 512 : p * 512 + KY, :] = ctf * wide[pl.ds(0, KY, stride=2), :]
        img_ref[p * 512 + KY : (p + 1) * 512, :] = ctf * wide[pl.ds(1, KY, stride=2), :]


CH = 64
BIG = 1024
PIECES = 2


def search_kernel(pos_ref, noise_ref, near_ref, far_ref, img_ref, sq_ref, fwd_ref, bwd_ref, corr_ref, back_ref,
                  sum_ref, far_out_ref, slots, rows_a, rows_b, q, row_phase, power, corr, weight):
    slots[0 : 2 * HALF, :] = near_ref[...].astype(F32)
    slots[2 * HALF : 4 * HALF, :] = far_ref[...].astype(F32)

    def fetch(r, rows, k):
        for y in range(k * CH, (k + 1) * CH):
            at = pl.multiple_of(pos_ref[r, y], 2)
            rows[2 * y : 2 * y + 2, :] = slots[pl.ds(at, 2), :]

    def put(r, rows, k):
        for y in range(k * CH, (k + 1) * CH):
            at = pl.multiple_of(pos_ref[r, y], 2)
            sum_ref[pl.ds(at, 2), :] = rows[2 * y : 2 * y + 2, :]

    def images(p, k):
        at = p * 512 + k * CH
        return img_ref[at : at + CH, :], img_ref[at + KY : at + KY + CH, :]

    def score_ref(r, rows, ahead, ahead_rows):
        sums = [jnp.zeros((8, KX), F32) for _ in range(PER)]
        for k in range(KY // CH):
            fetch(ahead, ahead_rows, k)
            re = rows[pl.ds(2 * CH * k, CH, stride=2), :]
            im = rows[pl.ds(2 * CH * k + 1, CH, stride=2), :]
            mag = re * re + im * im
            for p in range(PER):
                a_re, a_im = images(p, k)
                q[pl.ds(pl.multiple_of(r * KY + k * CH, CH), CH), p * 256 : p * 256 + 128] = (re * a_re + im * a_im).astype(BF16)
                q[pl.ds(pl.multiple_of(r * KY + k * CH, CH), CH), p * 256 + 128 : (p + 1) * 256] = (re * a_im - im * a_re).astype(BF16)
                part = sq_ref[p * KY + k * CH : p * KY + (k + 1) * CH, :] * mag
                sums[p] = sums[p] + jnp.sum(part.reshape(CH // 8, 8, KX), axis=0)
        for p in range(PER):
            power[pl.ds(p * REFS + r, 1), :] = jnp.sum(sums[p], axis=0, keepdims=True)

    def forward(t, carry):
        r = 2 * t
        score_ref(r, rows_a, r + 1, rows_b)
        score_ref(r + 1, rows_b, jnp.minimum(r + 2, REFS - 1), rows_a)
        return carry

    for k in range(KY // CH):
        fetch(0, rows_a, k)
    lax.fori_loop(0, REFS // 2, forward, 0)
    for m in range(ROWS // BIG):
        at = slice(m * BIG, (m + 1) * BIG)
        row_phase[at, :] = jnp.dot(q[at, :], fwd_ref[...], preferred_element_type=F32).astype(BF16)
    for r in range(REFS):
        both = jnp.dot(corr_ref[...], row_phase[r * KY : (r + 1) * KY, :], preferred_element_type=F32)
        corr[r * SHIFTS : (r + 1) * SHIFTS, :] = both[:SHIFTS, :128] - both[SHIFTS:, 128:]


    group = lax.shift_right_logical(iota((1, 128), 1), 5)
    noise = jnp.zeros((1, 128), F32)
    totals = jnp.zeros((REFS, 128), F32)
    for p in range(PER):
        noise = jnp.where(group == p, noise_ref[p], noise)
        column = jnp.sum(power[p * REFS : (p + 1) * REFS, :], axis=1, keepdims=True)
        totals = jnp.where(group == p, column, totals)
    score = corr[...].reshape(REFS, SHIFTS, 128) - 0.5 * totals[:, None, :]
    score = score.reshape(REFS * SHIFTS, 128) * noise
    top = jnp.max(score, axis=0, keepdims=True)
    peak = jnp.zeros((1, 128), F32)
    for p in range(PER):
        peak = jnp.where(group == p, jnp.max(jnp.where(group == p, top, -jnp.inf), axis=1, keepdims=True), peak)
    expo = jnp.exp(score - peak)
    lane_sum = jnp.sum(expo, axis=0, keepdims=True)
    norm = jnp.ones((1, 128), F32)
    for p in range(PER):
        norm = jnp.where(group == p, jnp.sum(jnp.where(group == p, lane_sum, 0.0), axis=1, keepdims=True), norm)
    weight[...] = (expo * (1.0 / norm)).astype(BF16)
    sum_ref[...] = jnp.zeros_like(sum_ref)

    def insert_ref(r, rows, behind, behind_rows):
        w = weight[pl.ds(pl.multiple_of(r * SHIFTS, SHIFTS), SHIFTS), :]
        col = jnp.dot(back_ref[...], w, preferred_element_type=F32).astype(BF16)
        col = jnp.concatenate([col[:KY], col[KY:]], axis=1)
        shifted = jnp.dot(col, bwd_ref[...], preferred_element_type=F32).astype(BF16)
        for k in range(KY // CH):
            put(behind, behind_rows, k)
            ss = shifted[k * CH : (k + 1) * CH].astype(F32)
            t_re = t_im = None
            for p in range(PER):
                a_re, a_im = images(p, k)
                s_re = ss[:, p * 256 : p * 256 + 128]
                s_im = ss[:, p * 256 + 128 : (p + 1) * 256]
                u_re = a_re * s_re - a_im * s_im
                u_im = a_re * s_im + a_im * s_re
                t_re = u_re if t_re is None else t_re + u_re
                t_im = u_im if t_im is None else t_im + u_im
            rows[pl.ds(2 * CH * k, CH, stride=2), :] = t_re
            rows[pl.ds(2 * CH * k + 1, CH, stride=2), :] = t_im

    def backward(t, carry):
        r = 2 * t
        insert_ref(r, rows_a, (r + REFS - 1) % REFS, rows_b)
        insert_ref(r + 1, rows_b, r, rows_a)
        return carry

    lax.fori_loop(0, REFS // 2, backward, 0)
    for k in range(KY // CH):
        put(REFS - 1, rows_b, k)
    far_out_ref[...] = sum_ref[2 * HALF : 4 * HALF, :].astype(BF16)


def insert_kernel(mine_ref, got_ref, out_hbm, wide, left, right, out, sems):
    hi_iota = iota((512, 128), 0)
    lo_iota = iota((128, 128), 0)
    sums = jnp.sum(got_ref[...].astype(F32).reshape(32, 24, 128), axis=0)
    wide[...] = sums * (1.0 / math.sqrt(PARTICLES))
    for k in range(CAP):
        vox = mine_ref[k : k + 1, :]
        at = slice(k * 128, (k + 1) * 128)
        left[:, at] = (hi_iota == lax.shift_right_arithmetic(vox, 7)).astype(F32).astype(BF16)
        here = lo_iota == (vox & 127)
        for c in range(2):
            total = wide[2 * k + c : 2 * k + c + 1, :] + wide[12 + 2 * k + c : 12 + 2 * k + c + 1, :]
            first = total.astype(BF16).astype(F32)
            right[c * 256 : c * 256 + 128, at] = jnp.where(here, first, 0.0).astype(BF16)
            right[c * 256 + 128 : c * 256 + 256, at] = jnp.where(here, total - first, 0.0).astype(BF16)
    size = 512 // PIECES
    stores = []
    for m in range(PIECES):
        both = lax.dot_general(
            left[m * size : (m + 1) * size, :], right[...], (((1,), (1,)), ((), ())), preferred_element_type=F32
        )
        for c in range(2):
            out[pl.ds(2 * size * m + c, size, stride=2), :] = (
                both[:, c * 256 : c * 256 + 128] + both[:, c * 256 + 128 : c * 256 + 256]
            )
        at = pl.ds(2 * size * m, 2 * size)
        stores.append(pltpu.make_async_copy(out.at[at, :], out_hbm.at[at, :], sems.at[m]))
        stores[m].start()
    for store in stores:
        store.wait()


def pair_kernel(sums_ref, got_ref, out_ref):
    out_ref[...] = (sums_ref[0 : 2 * HALF, :] + got_ref[...].astype(F32)).astype(BF16)


def line_kernel(got_ref, out_ref):
    total = got_ref[0:768, :].astype(F32)
    for k in range(1, 4):
        total = total + got_ref[k * 768 : (k + 1) * 768, :].astype(F32)
    out_ref[...] = total.astype(BF16)


VM = pl.BlockSpec(memory_space=pltpu.VMEM)
SM = pl.BlockSpec(memory_space=pltpu.SMEM)
ANY = pl.BlockSpec(memory_space=pl.ANY)


def shape(dims, dtype):
    return jax.ShapeDtypeStruct(dims, dtype)


def params():
    return pltpu.CompilerParams(vmem_limit_bytes=VMEM_LIMIT)


def cost(us):
    return pl.CostEstimate(flops=int(us * 1e9), bytes_accessed=int(us * 1e6), transcendentals=0)


def pick_call(me, owner, volume_rows, voxel_rows):
    return pl.pallas_call(
        pick_kernel,
        out_shape=(
            shape((REFS, KY), jnp.int32),
            shape((8, 128), jnp.int32),
            shape((64 * 12, 128), BF16),
        ),
        in_specs=[SM, ANY, ANY, ANY],
        out_specs=(VM, VM, VM),
        scratch_shapes=[
            pltpu.VMEM((REFS, KY), jnp.int32),
            pltpu.VMEM((REFS, KY), jnp.int32),
            pltpu.VMEM((96, 128), F32),
            pltpu.VMEM((1024, 128), BF16),
            pltpu.VMEM((ROWS, KX), jnp.int32),
            pltpu.SemaphoreType.DMA((3,)),
        ],
        compiler_params=pltpu.CompilerParams(vmem_limit_bytes=107 * 512 * 1024),
        name="pick_rows",
    )(me, owner, volume_rows, voxel_rows)


def image_call(defocus, particle_rows):
    return pl.pallas_call(
        image_kernel,
        out_shape=(shape((PER * 512, KX), F32), shape((PER * KY, KX), F32)),
        in_specs=[SM, VM],
        out_specs=(VM, VM),
        scratch_shapes=[pltpu.VMEM((512, KX), F32)],
        compiler_params=params(),
        cost_estimate=cost(4),
        name="ctf_images",
    )(defocus, particle_rows)


def search_call(pos, noise, near, far, img, sq):
    tables = [jnp.asarray(t) for t in phase_constants()]
    return pl.pallas_call(
        search_kernel,
        out_shape=(shape((4 * HALF, KX), F32), shape((2 * HALF, KX), BF16)),
        in_specs=[SM, SM] + [VM] * 8,
        out_specs=(VM, VM),
        scratch_shapes=[
            pltpu.VMEM((4 * HALF, KX), F32),
            pltpu.VMEM((2 * KY, KX), F32),
            pltpu.VMEM((2 * KY, KX), F32),
            pltpu.VMEM((REFS * KY, PER * 2 * KX), BF16),
            pltpu.VMEM((REFS * KY, 2 * PER * SHIFTS), BF16),
            pltpu.VMEM((PER * REFS, KX), F32),
            pltpu.VMEM((REFS * SHIFTS, 128), F32),
            pltpu.VMEM((REFS * SHIFTS, 128), BF16),
        ],
        compiler_params=params(),
        name="shift_search",
    )(pos, noise, near, far, img, sq, *tables)


def small_call(kernel, name, rows, *args):
    return pl.pallas_call(
        kernel,
        out_shape=shape((rows, 128), BF16),
        in_specs=[VM] * len(args),
        out_specs=VM,
        compiler_params=params(),
        name=name,
    )(*args)


def insert_call(mine, got):
    return pl.pallas_call(
        insert_kernel,
        out_shape=shape((1024, 128), F32),
        in_specs=[VM, VM],
        out_specs=ANY,
        scratch_shapes=[
            pltpu.VMEM((24, 128), F32),
            pltpu.VMEM((512, CAP * 128), BF16),
            pltpu.VMEM((512, CAP * 128), BF16),
            pltpu.VMEM((1024, 128), F32),
            pltpu.SemaphoreType.DMA((PIECES,)),
        ],
        compiler_params=params(),
        name="insert_rows",
    )(mine, got)


def local(particles, defocus, inverse_noise, volume, slice_owner, slice_voxel):
    me = lax.axis_index(FINE).astype(jnp.int32).reshape(1)
    volume_rows = volume.reshape(2, 512, 128).transpose(1, 0, 2).reshape(1024, 128)
    pos, mine, compact = pick_call(me, slice_owner, volume_rows, slice_voxel.reshape(ROWS, KX))
    line = lax.all_to_all(compact.reshape(64, CAP, 2, 128), ("zh", "zl", "y"), 0, 0, tiled=True)
    spread = jnp.broadcast_to(line.reshape(1, 384, 2, 128), (4, 384, 2, 128))
    near = lax.all_to_all(spread, "x", 0, 0, tiled=True).reshape(HALF, 2, 128)
    swap = [(0, 1), (1, 0)]
    far = lax.ppermute(near, "c", swap)
    img, sq = image_call(defocus, particles.reshape(PER * KY * 2, KX))
    sums, far_out = search_call(
        pos, inverse_noise, near.reshape(2 * HALF, 128), far.reshape(2 * HALF, 128), img, sq
    )
    received = lax.ppermute(far_out.reshape(HALF, 2, 128), "c", swap)
    pair = small_call(pair_kernel, "add_core", 2 * HALF, sums, received.reshape(2 * HALF, 128))
    plane = lax.all_to_all(pair.reshape(4, 384, 2, 128), "x", 0, 0, tiled=True)
    plane = small_call(line_kernel, "add_line", 768, plane.reshape(2 * HALF, 128))
    last = lax.all_to_all(plane.reshape(64, CAP, 2, 128), ("zh", "zl", "y"), 0, 0, tiled=True)
    out = insert_call(mine, last.reshape(768, 128))
    return out.reshape(512, 2, 128).transpose(1, 0, 2).reshape(2, 65536)


def solution(mesh):
    fine = Mesh(mesh.devices.reshape(4, 2, 8, 4, 2), FINE)
    in_specs = (P(FINE, None, None, None), P(FINE), P(FINE), P(None, FINE), P(), P())
    return jax.shard_map(local, mesh=fine, in_specs=in_specs, out_specs=P(None, FINE), check_vma=False)
```

```python
import math

import jax
import jax.numpy as jnp
import ml_dtypes
import numpy as np
from jax import lax
from jax.experimental import pallas as pl
from jax.experimental.pallas import tpu as pltpu
from jax.sharding import Mesh
from jax.sharding import PartitionSpec as P

KY, KX, REFS, SHIFTS, CAP, PER = 256, 128, 8, 32, 6, 4
ROWS = REFS * KY
PARTICLES = 2048
HALF = 1536
BOX = 400
WAVE = 0.0197
AMP = 0.1
VMEM_LIMIT = 40 * 1024 * 1024
FINE = ("zh", "c", "y", "x", "zl")
F32 = jnp.float32
BF16 = jnp.bfloat16


def phase_constants():
    shift = np.arange(SHIFTS) - SHIFTS // 2
    fy = np.arange(KY) - KY // 2
    fx = np.arange(KX)
    ang_y = 2.0 * np.pi / BOX * np.mod(fy[:, None] * shift[None, :], BOX)
    ang_x = 2.0 * np.pi / BOX * np.mod(fx[:, None] * shift[None, :], BOX)
    cos_y, sin_y, cos_x, sin_x = np.cos(ang_y), np.sin(ang_y), np.cos(ang_x), np.sin(ang_x)
    fwd = np.zeros((PER, 2, KX, 2, PER, SHIFTS))
    bwd = np.zeros((2, PER, SHIFTS, PER, 2, KX))
    for p in range(PER):
        fwd[p, 0, :, 0, p], fwd[p, 0, :, 1, p] = cos_x, sin_x
        fwd[p, 1, :, 0, p], fwd[p, 1, :, 1, p] = -sin_x, cos_x
        bwd[0, p, :, p, 0], bwd[0, p, :, p, 1] = cos_x.T, sin_x.T
        bwd[1, p, :, p, 0], bwd[1, p, :, p, 1] = -sin_x.T, cos_x.T
    fwd = fwd.reshape(PER * 2 * KX, 2 * PER * SHIFTS)
    bwd = bwd.reshape(2 * PER * SHIFTS, PER * 2 * KX)
    corr = np.concatenate([cos_y.T, sin_y.T], axis=0)
    back = np.concatenate([cos_y, sin_y], axis=0)
    return [a.astype(np.float32).astype(ml_dtypes.bfloat16) for a in (fwd, bwd, corr, back)]


def iota(shape, dim):
    return lax.broadcasted_iota(jnp.int32, shape, dim)


def pick_kernel(me_ref, own_hbm, vol_hbm, vox_hbm, pos_ref, mine_ref, out_ref, owners, slot, stage, table, voxels, sems):
    load_own = pltpu.make_async_copy(own_hbm, owners, sems.at[0])
    load_vox = pltpu.make_async_copy(vox_hbm, voxels, sems.at[1])
    load_vol = pltpu.make_async_copy(vol_hbm, table, sems.at[2])
    load_own.start()
    load_vox.start()
    load_vol.start()
    me = me_ref[0]
    load_own.wait()
    own = owners[...]
    turned = own.astype(F32).T
    cols, here = [], []
    for b in range(ROWS // 128):
        r, h = b // 2, b % 2
        cols.append(jnp.broadcast_to(turned[h * 128 : (h + 1) * 128, r : r + 1], (128, 128)))
        here.append(jnp.broadcast_to(own[r : r + 1, h * 128 : (h + 1) * 128].astype(F32), (128, 128)))
    earlier = iota((128, 128), 0) < iota((128, 128), 1)
    for b in range(ROWS // 128):
        r, h = b // 2, b % 2
        hits = ((cols[b] == here[b]) & earlier).astype(F32)
        for c in range(b):
            hits = hits + (cols[c] == here[b]).astype(F32)
        slot[r : r + 1, h * 128 : (h + 1) * 128] = jnp.sum(hits, axis=0, keepdims=True).astype(jnp.int32)
    slots = slot[...]
    row_id = iota((REFS, KY), 0) * KY + iota((REFS, KY), 1)
    is_me = own == me
    found = [jnp.max(jnp.where(is_me & (slots == k), row_id, -1)) for k in range(CAP)]
    z = lax.shift_right_logical(own, 7)
    y = lax.shift_right_logical(own, 3) & 7
    x = lax.shift_right_logical(own, 1) & 3
    across = ((lax.shift_right_logical(own, 6) ^ lax.shift_right_logical(me, 6)) & 1) * HALF
    pos_ref[...] = 2 * (across + (x * 2 + (own & 1)) * (32 * CAP) + (z * 8 + y) * CAP + jnp.minimum(slots, CAP - 1))
    parity = (iota((8, 128), 0) & 1) == 0
    row_pair = lax.shift_right_logical(iota((1024, 128), 0), 1)
    lo_iota = iota((128, 128), 0)
    mine_ref[...] = jnp.full((8, 128), -1, jnp.int32)
    load_vox.wait()
    load_vol.wait()
    for k in range(CAP):
        vox = voxels[pl.ds(jnp.maximum(found[k], 0), 1), :]
        vox = jnp.where(found[k] >= 0, vox, -1)
        mine_ref[k : k + 1, :] = vox
        hi = lax.shift_right_arithmetic(vox, 7)
        onehot = (lo_iota == (vox & 127)).astype(F32).astype(BF16)
        wide = jnp.dot(table[...], onehot, preferred_element_type=F32)
        kept = jnp.where(row_pair == hi, wide, 0.0)
        kept = jnp.sum(kept.reshape(128, 8, 128), axis=0)
        re = jnp.sum(jnp.where(parity, kept, 0.0), axis=0, keepdims=True)
        im = jnp.sum(jnp.where(parity, 0.0, kept), axis=0, keepdims=True)
        for copy in range(8):
            stage[copy * 12 + 2 * k : copy * 12 + 2 * k + 1, :] = re
            stage[copy * 12 + 2 * k + 1 : copy * 12 + 2 * k + 2, :] = im
    block = stage[...].astype(BF16)
    for copy in range(4):
        out_ref[copy * 96 : (copy + 1) * 96, :] = block


def image_kernel(defocus_ref, part_ref, img_ref, sq_ref, wide):
    fy = (iota((KY, KX), 0) - KY // 2).astype(F32)
    fx = iota((KY, KX), 1).astype(F32)
    radius = (fy * fy + fx * fx) / float(BOX * BOX)
    phase0 = math.asin(AMP)
    pi_a = 3.140625
    pi_b = 9.67502593994140625e-4
    pi_c = math.pi - pi_a - pi_b
    coef = [(-1.0) ** k / math.factorial(2 * k + 1) for k in range(7)]
    for p in range(PER):
        wide[...] = part_ref[p * 512 : (p + 1) * 512, :].astype(F32)
        chi = (math.pi * WAVE * defocus_ref[p]) * radius
        whole = jnp.floor(chi * (1.0 / math.pi) + (phase0 / math.pi + 0.5))
        frac = ((chi - whole * pi_a) - whole * pi_b) - (whole * pi_c - phase0)
        half = whole * 0.5
        frac = frac * (1.0 - 4.0 * (half - jnp.floor(half)))
        sq = frac * frac
        poly = jnp.full_like(sq, coef[6])
        for k in range(5, -1, -1):
            poly = poly * sq + coef[k]
        ctf = -(poly * frac)
        sq_ref[p * KY : (p + 1) * KY, :] = ctf * ctf
        img_ref[p * 512 : p * 512 + KY, :] = ctf * wide[pl.ds(0, KY, stride=2), :]
        img_ref[p * 512 + KY : (p + 1) * 512, :] = ctf * wide[pl.ds(1, KY, stride=2), :]


CH = 64
BIG = 1024
PIECES = 2


def search_kernel(pos_ref, noise_ref, near_ref, far_ref, img_ref, sq_ref, fwd_ref, bwd_ref, corr_ref, back_ref,
                  sum_ref, far_out_ref, slots, rows_a, rows_b, q, row_phase, power, corr, weight):
    slots[0 : 2 * HALF, :] = near_ref[...].astype(F32)
    slots[2 * HALF : 4 * HALF, :] = far_ref[...].astype(F32)

    def fetch(r, rows, k):
        for y in range(k * CH, (k + 1) * CH):
            at = pl.multiple_of(pos_ref[r, y], 2)
            rows[2 * y : 2 * y + 2, :] = slots[pl.ds(at, 2), :]

    def put(r, rows, k):
        for y in range(k * CH, (k + 1) * CH):
            at = pl.multiple_of(pos_ref[r, y], 2)
            sum_ref[pl.ds(at, 2), :] = rows[2 * y : 2 * y + 2, :]

    def images(p, k):
        at = p * 512 + k * CH
        return img_ref[at : at + CH, :], img_ref[at + KY : at + KY + CH, :]

    def score_ref(r, rows, ahead, ahead_rows):
        sums = [jnp.zeros((8, KX), F32) for _ in range(PER)]
        for k in range(KY // CH):
            fetch(ahead, ahead_rows, k)
            re = rows[pl.ds(2 * CH * k, CH, stride=2), :]
            im = rows[pl.ds(2 * CH * k + 1, CH, stride=2), :]
            mag = re * re + im * im
            for p in range(PER):
                a_re, a_im = images(p, k)
                q[pl.ds(pl.multiple_of(r * KY + k * CH, CH), CH), p * 256 : p * 256 + 128] = (re * a_re + im * a_im).astype(BF16)
                q[pl.ds(pl.multiple_of(r * KY + k * CH, CH), CH), p * 256 + 128 : (p + 1) * 256] = (re * a_im - im * a_re).astype(BF16)
                part = sq_ref[p * KY + k * CH : p * KY + (k + 1) * CH, :] * mag
                sums[p] = sums[p] + jnp.sum(part.reshape(CH // 8, 8, KX), axis=0)
        for p in range(PER):
            power[pl.ds(p * REFS + r, 1), :] = jnp.sum(sums[p], axis=0, keepdims=True)

    def forward(t, carry):
        r = 2 * t
        score_ref(r, rows_a, r + 1, rows_b)
        score_ref(r + 1, rows_b, jnp.minimum(r + 2, REFS - 1), rows_a)
        return carry

    for k in range(KY // CH):
        fetch(0, rows_a, k)
    lax.fori_loop(0, REFS // 2, forward, 0)
    for m in range(ROWS // BIG):
        at = slice(m * BIG, (m + 1) * BIG)
        row_phase[at, :] = jnp.dot(q[at, :], fwd_ref[...], preferred_element_type=F32).astype(BF16)
    for r in range(REFS):
        both = jnp.dot(corr_ref[...], row_phase[r * KY : (r + 1) * KY, :], preferred_element_type=F32)
        corr[r * SHIFTS : (r + 1) * SHIFTS, :] = both[:SHIFTS, :128] - both[SHIFTS:, 128:]


    group = lax.shift_right_logical(iota((1, 128), 1), 5)
    noise = jnp.zeros((1, 128), F32)
    totals = jnp.zeros((REFS, 128), F32)
    for p in range(PER):
        noise = jnp.where(group == p, noise_ref[p], noise)
        column = jnp.sum(power[p * REFS : (p + 1) * REFS, :], axis=1, keepdims=True)
        totals = jnp.where(group == p, column, totals)
    score = corr[...].reshape(REFS, SHIFTS, 128) - 0.5 * totals[:, None, :]
    score = score.reshape(REFS * SHIFTS, 128) * noise
    top = jnp.max(score, axis=0, keepdims=True)
    peak = jnp.zeros((1, 128), F32)
    for p in range(PER):
        peak = jnp.where(group == p, jnp.max(jnp.where(group == p, top, -jnp.inf), axis=1, keepdims=True), peak)
    expo = jnp.exp(score - peak)
    lane_sum = jnp.sum(expo, axis=0, keepdims=True)
    norm = jnp.ones((1, 128), F32)
    for p in range(PER):
        norm = jnp.where(group == p, jnp.sum(jnp.where(group == p, lane_sum, 0.0), axis=1, keepdims=True), norm)
    weight[...] = (expo * (1.0 / norm)).astype(BF16)
    sum_ref[...] = jnp.zeros_like(sum_ref)

    def insert_ref(r, rows, behind, behind_rows):
        w = weight[pl.ds(pl.multiple_of(r * SHIFTS, SHIFTS), SHIFTS), :]
        col = jnp.dot(back_ref[...], w, preferred_element_type=F32).astype(BF16)
        col = jnp.concatenate([col[:KY], col[KY:]], axis=1)
        shifted = jnp.dot(col, bwd_ref[...], preferred_element_type=F32).astype(BF16)
        for k in range(KY // CH):
            put(behind, behind_rows, k)
            ss = shifted[k * CH : (k + 1) * CH].astype(F32)
            t_re = t_im = None
            for p in range(PER):
                a_re, a_im = images(p, k)
                s_re = ss[:, p * 256 : p * 256 + 128]
                s_im = ss[:, p * 256 + 128 : (p + 1) * 256]
                u_re = a_re * s_re - a_im * s_im
                u_im = a_re * s_im + a_im * s_re
                t_re = u_re if t_re is None else t_re + u_re
                t_im = u_im if t_im is None else t_im + u_im
            rows[pl.ds(2 * CH * k, CH, stride=2), :] = t_re
            rows[pl.ds(2 * CH * k + 1, CH, stride=2), :] = t_im

    def backward(t, carry):
        r = 2 * t
        insert_ref(r, rows_a, (r + REFS - 1) % REFS, rows_b)
        insert_ref(r + 1, rows_b, r, rows_a)
        return carry

    lax.fori_loop(0, REFS // 2, backward, 0)
    for k in range(KY // CH):
        put(REFS - 1, rows_b, k)
    far_out_ref[...] = sum_ref[2 * HALF : 4 * HALF, :].astype(BF16)


def insert_kernel(mine_ref, got_ref, out_hbm, wide, left, right, out, sems):
    hi_iota = iota((512, 128), 0)
    lo_iota = iota((128, 128), 0)
    sums = jnp.sum(got_ref[...].astype(F32).reshape(16, 24, 128), axis=0)
    wide[...] = sums * (1.0 / math.sqrt(PARTICLES))
    for k in range(CAP):
        vox = mine_ref[k : k + 1, :]
        at = slice(k * 128, (k + 1) * 128)
        left[:, at] = (hi_iota == lax.shift_right_arithmetic(vox, 7)).astype(F32).astype(BF16)
        here = lo_iota == (vox & 127)
        for c in range(2):
            total = wide[2 * k + c : 2 * k + c + 1, :] + wide[12 + 2 * k + c : 12 + 2 * k + c + 1, :]
            first = total.astype(BF16).astype(F32)
            right[c * 256 : c * 256 + 128, at] = jnp.where(here, first, 0.0).astype(BF16)
            right[c * 256 + 128 : c * 256 + 256, at] = jnp.where(here, total - first, 0.0).astype(BF16)
    size = 512 // PIECES
    stores = []
    for m in range(PIECES):
        both = lax.dot_general(
            left[m * size : (m + 1) * size, :], right[...], (((1,), (1,)), ((), ())), preferred_element_type=F32
        )
        for c in range(2):
            out[pl.ds(2 * size * m + c, size, stride=2), :] = (
                both[:, c * 256 : c * 256 + 128] + both[:, c * 256 + 128 : c * 256 + 256]
            )
        at = pl.ds(2 * size * m, 2 * size)
        stores.append(pltpu.make_async_copy(out.at[at, :], out_hbm.at[at, :], sems.at[m]))
        stores[m].start()
    for store in stores:
        store.wait()


def pair_kernel(sums_ref, got_ref, out_ref):
    out_ref[...] = (sums_ref[0 : 2 * HALF, :] + got_ref[...].astype(F32)).astype(BF16)


def line_kernel(got_ref, out_ref):
    total = got_ref[0:384, :].astype(F32)
    for k in range(1, 8):
        total = total + got_ref[k * 384 : (k + 1) * 384, :].astype(F32)
    out_ref[...] = total.astype(BF16)


VM = pl.BlockSpec(memory_space=pltpu.VMEM)
SM = pl.BlockSpec(memory_space=pltpu.SMEM)
ANY = pl.BlockSpec(memory_space=pl.ANY)


def shape(dims, dtype):
    return jax.ShapeDtypeStruct(dims, dtype)


def params():
    return pltpu.CompilerParams(vmem_limit_bytes=VMEM_LIMIT)


def cost(us):
    return pl.CostEstimate(flops=int(us * 1e9), bytes_accessed=int(us * 1e6), transcendentals=0)


def pick_call(me, owner, volume_rows, voxel_rows):
    return pl.pallas_call(
        pick_kernel,
        out_shape=(
            shape((REFS, KY), jnp.int32),
            shape((8, 128), jnp.int32),
            shape((32 * 12, 128), BF16),
        ),
        in_specs=[SM, ANY, ANY, ANY],
        out_specs=(VM, VM, VM),
        scratch_shapes=[
            pltpu.VMEM((REFS, KY), jnp.int32),
            pltpu.VMEM((REFS, KY), jnp.int32),
            pltpu.VMEM((96, 128), F32),
            pltpu.VMEM((1024, 128), BF16),
            pltpu.VMEM((ROWS, KX), jnp.int32),
            pltpu.SemaphoreType.DMA((3,)),
        ],
        compiler_params=pltpu.CompilerParams(vmem_limit_bytes=107 * 512 * 1024),
        name="pick_rows",
    )(me, owner, volume_rows, voxel_rows)


def image_call(defocus, particle_rows):
    return pl.pallas_call(
        image_kernel,
        out_shape=(shape((PER * 512, KX), F32), shape((PER * KY, KX), F32)),
        in_specs=[SM, VM],
        out_specs=(VM, VM),
        scratch_shapes=[pltpu.VMEM((512, KX), F32)],
        compiler_params=params(),
        cost_estimate=cost(4),
        name="ctf_images",
    )(defocus, particle_rows)


def search_call(pos, noise, near, far, img, sq):
    tables = [jnp.asarray(t) for t in phase_constants()]
    return pl.pallas_call(
        search_kernel,
        out_shape=(shape((4 * HALF, KX), F32), shape((2 * HALF, KX), BF16)),
        in_specs=[SM, SM] + [VM] * 8,
        out_specs=(VM, VM),
        scratch_shapes=[
            pltpu.VMEM((4 * HALF, KX), F32),
            pltpu.VMEM((2 * KY, KX), F32),
            pltpu.VMEM((2 * KY, KX), F32),
            pltpu.VMEM((REFS * KY, PER * 2 * KX), BF16),
            pltpu.VMEM((REFS * KY, 2 * PER * SHIFTS), BF16),
            pltpu.VMEM((PER * REFS, KX), F32),
            pltpu.VMEM((REFS * SHIFTS, 128), F32),
            pltpu.VMEM((REFS * SHIFTS, 128), BF16),
        ],
        compiler_params=params(),
        name="shift_search",
    )(pos, noise, near, far, img, sq, *tables)


def small_call(kernel, name, rows, *args):
    return pl.pallas_call(
        kernel,
        out_shape=shape((rows, 128), BF16),
        in_specs=[VM] * len(args),
        out_specs=VM,
        compiler_params=params(),
        name=name,
    )(*args)


def insert_call(mine, got):
    return pl.pallas_call(
        insert_kernel,
        out_shape=shape((1024, 128), F32),
        in_specs=[VM, VM],
        out_specs=ANY,
        scratch_shapes=[
            pltpu.VMEM((24, 128), F32),
            pltpu.VMEM((512, CAP * 128), BF16),
            pltpu.VMEM((512, CAP * 128), BF16),
            pltpu.VMEM((1024, 128), F32),
            pltpu.SemaphoreType.DMA((PIECES,)),
        ],
        compiler_params=params(),
        name="insert_rows",
    )(mine, got)


def local(particles, defocus, inverse_noise, volume, slice_owner, slice_voxel):
    me = lax.axis_index(FINE).astype(jnp.int32).reshape(1)
    volume_rows = volume.reshape(2, 512, 128).transpose(1, 0, 2).reshape(1024, 128)
    pos, mine, compact = pick_call(me, slice_owner, volume_rows, slice_voxel.reshape(ROWS, KX))
    line = lax.all_to_all(compact.reshape(32, CAP, 2, 128), ("zh", "y"), 0, 0, tiled=True)
    spread = jnp.broadcast_to(line.reshape(1, 192, 2, 128), (8, 192, 2, 128))
    near = lax.all_to_all(spread, ("x", "zl"), 0, 0, tiled=True).reshape(HALF, 2, 128)
    swap = [(0, 1), (1, 0)]
    far = lax.ppermute(near, "c", swap)
    img, sq = image_call(defocus, particles.reshape(PER * KY * 2, KX))
    sums, far_out = search_call(
        pos, inverse_noise, near.reshape(2 * HALF, 128), far.reshape(2 * HALF, 128), img, sq
    )
    received = lax.ppermute(far_out.reshape(HALF, 2, 128), "c", swap)
    pair = small_call(pair_kernel, "add_core", 2 * HALF, sums, received.reshape(2 * HALF, 128))
    plane = lax.all_to_all(pair.reshape(8, 192, 2, 128), ("x", "zl"), 0, 0, tiled=True)
    plane = small_call(line_kernel, "add_line", 384, plane.reshape(2 * HALF, 128))
    last = lax.all_to_all(plane.reshape(32, CAP, 2, 128), ("zh", "y"), 0, 0, tiled=True)
    out = insert_call(mine, last.reshape(384, 128))
    return out.reshape(512, 2, 128).transpose(1, 0, 2).reshape(2, 65536)


def solution(mesh):
    fine = Mesh(mesh.devices.reshape(4, 2, 8, 4, 2), FINE)
    in_specs = (P(FINE, None, None, None), P(FINE), P(FINE), P(None, FINE), P(), P())
    return jax.shard_map(local, mesh=fine, in_specs=in_specs, out_specs=P(None, FINE), check_vma=False)
```

```python
import math

import jax
import jax.numpy as jnp
import ml_dtypes
import numpy as np
from jax import lax
from jax.experimental import pallas as pl
from jax.experimental.pallas import tpu as pltpu
from jax.sharding import Mesh
from jax.sharding import PartitionSpec as P

KY, KX, REFS, SHIFTS, CAP, PER = 256, 128, 8, 32, 6, 4
ROWS = REFS * KY
PARTICLES = 2048
HALF = 1536
BOX = 400
WAVE = 0.0197
AMP = 0.1
VMEM_LIMIT = 40 * 1024 * 1024
FINE = ("zh", "c", "yh", "yl", "x", "zl")
F32 = jnp.float32
BF16 = jnp.bfloat16


def phase_constants():
    shift = np.arange(SHIFTS) - SHIFTS // 2
    fy = np.arange(KY) - KY // 2
    fx = np.arange(KX)
    ang_y = 2.0 * np.pi / BOX * np.mod(fy[:, None] * shift[None, :], BOX)
    ang_x = 2.0 * np.pi / BOX * np.mod(fx[:, None] * shift[None, :], BOX)
    cos_y, sin_y, cos_x, sin_x = np.cos(ang_y), np.sin(ang_y), np.cos(ang_x), np.sin(ang_x)
    fwd = np.zeros((PER, 2, KX, 2, PER, SHIFTS))
    bwd = np.zeros((2, PER, SHIFTS, PER, 2, KX))
    for p in range(PER):
        fwd[p, 0, :, 0, p], fwd[p, 0, :, 1, p] = cos_x, sin_x
        fwd[p, 1, :, 0, p], fwd[p, 1, :, 1, p] = -sin_x, cos_x
        bwd[0, p, :, p, 0], bwd[0, p, :, p, 1] = cos_x.T, sin_x.T
        bwd[1, p, :, p, 0], bwd[1, p, :, p, 1] = -sin_x.T, cos_x.T
    fwd = fwd.reshape(PER * 2 * KX, 2 * PER * SHIFTS)
    bwd = bwd.reshape(2 * PER * SHIFTS, PER * 2 * KX)
    corr = np.concatenate([cos_y.T, sin_y.T], axis=0)
    back = np.concatenate([cos_y, sin_y], axis=0)
    return [a.astype(np.float32).astype(ml_dtypes.bfloat16) for a in (fwd, bwd, corr, back)]


def iota(shape, dim):
    return lax.broadcasted_iota(jnp.int32, shape, dim)


def pick_kernel(me_ref, own_hbm, vol_hbm, vox_hbm, pos_ref, mine_ref, out_ref, owners, slot, stage, table, voxels, sems):
    load_own = pltpu.make_async_copy(own_hbm, owners, sems.at[0])
    load_vox = pltpu.make_async_copy(vox_hbm, voxels, sems.at[1])
    load_vol = pltpu.make_async_copy(vol_hbm, table, sems.at[2])
    load_own.start()
    load_vox.start()
    load_vol.start()
    me = me_ref[0]
    load_own.wait()
    own = owners[...]
    turned = own.astype(F32).T
    cols, here = [], []
    for b in range(ROWS // 128):
        r, h = b // 2, b % 2
        cols.append(jnp.broadcast_to(turned[h * 128 : (h + 1) * 128, r : r + 1], (128, 128)))
        here.append(jnp.broadcast_to(own[r : r + 1, h * 128 : (h + 1) * 128].astype(F32), (128, 128)))
    earlier = iota((128, 128), 0) < iota((128, 128), 1)
    for b in range(ROWS // 128):
        r, h = b // 2, b % 2
        hits = ((cols[b] == here[b]) & earlier).astype(F32)
        for c in range(b):
            hits = hits + (cols[c] == here[b]).astype(F32)
        slot[r : r + 1, h * 128 : (h + 1) * 128] = jnp.sum(hits, axis=0, keepdims=True).astype(jnp.int32)
    slots = slot[...]
    row_id = iota((REFS, KY), 0) * KY + iota((REFS, KY), 1)
    is_me = own == me
    found = [jnp.max(jnp.where(is_me & (slots == k), row_id, -1)) for k in range(CAP)]
    z = lax.shift_right_logical(own, 7)
    y = lax.shift_right_logical(own, 3) & 7
    x = lax.shift_right_logical(own, 1) & 3
    across = ((lax.shift_right_logical(own, 6) ^ lax.shift_right_logical(me, 6)) & 1) * HALF
    pos_ref[...] = 2 * (across + (x * 4 + (own & 1) * 2 + (y & 1)) * (16 * CAP) + (z * 4 + lax.shift_right_logical(y, 1)) * CAP + jnp.minimum(slots, CAP - 1))
    parity = (iota((8, 128), 0) & 1) == 0
    row_pair = lax.shift_right_logical(iota((1024, 128), 0), 1)
    lo_iota = iota((128, 128), 0)
    mine_ref[...] = jnp.full((8, 128), -1, jnp.int32)
    load_vox.wait()
    load_vol.wait()
    for k in range(CAP):
        vox = voxels[pl.ds(jnp.maximum(found[k], 0), 1), :]
        vox = jnp.where(found[k] >= 0, vox, -1)
        mine_ref[k : k + 1, :] = vox
        hi = lax.shift_right_arithmetic(vox, 7)
        onehot = (lo_iota == (vox & 127)).astype(F32).astype(BF16)
        wide = jnp.dot(table[...], onehot, preferred_element_type=F32)
        kept = jnp.where(row_pair == hi, wide, 0.0)
        kept = jnp.sum(kept.reshape(128, 8, 128), axis=0)
        re = jnp.sum(jnp.where(parity, kept, 0.0), axis=0, keepdims=True)
        im = jnp.sum(jnp.where(parity, 0.0, kept), axis=0, keepdims=True)
        for copy in range(8):
            stage[copy * 12 + 2 * k : copy * 12 + 2 * k + 1, :] = re
            stage[copy * 12 + 2 * k + 1 : copy * 12 + 2 * k + 2, :] = im
    block = stage[...].astype(BF16)
    for copy in range(2):
        out_ref[copy * 96 : (copy + 1) * 96, :] = block


def image_kernel(defocus_ref, part_ref, img_ref, sq_ref, wide):
    fy = (iota((KY, KX), 0) - KY // 2).astype(F32)
    fx = iota((KY, KX), 1).astype(F32)
    radius = (fy * fy + fx * fx) / float(BOX * BOX)
    phase0 = math.asin(AMP)
    pi_a = 3.140625
    pi_b = 9.67502593994140625e-4
    pi_c = math.pi - pi_a - pi_b
    coef = [(-1.0) ** k / math.factorial(2 * k + 1) for k in range(7)]
    for p in range(PER):
        wide[...] = part_ref[p * 512 : (p + 1) * 512, :].astype(F32)
        chi = (math.pi * WAVE * defocus_ref[p]) * radius
        whole = jnp.floor(chi * (1.0 / math.pi) + (phase0 / math.pi + 0.5))
        frac = ((chi - whole * pi_a) - whole * pi_b) - (whole * pi_c - phase0)
        half = whole * 0.5
        frac = frac * (1.0 - 4.0 * (half - jnp.floor(half)))
        sq = frac * frac
        poly = jnp.full_like(sq, coef[6])
        for k in range(5, -1, -1):
            poly = poly * sq + coef[k]
        ctf = -(poly * frac)
        sq_ref[p * KY : (p + 1) * KY, :] = ctf * ctf
        img_ref[p * 512 : p * 512 + KY, :] = ctf * wide[pl.ds(0, KY, stride=2), :]
        img_ref[p * 512 + KY : (p + 1) * 512, :] = ctf * wide[pl.ds(1, KY, stride=2), :]


CH = 64
BIG = 1024
PIECES = 2


def search_kernel(pos_ref, noise_ref, near_ref, far_ref, img_ref, sq_ref, fwd_ref, bwd_ref, corr_ref, back_ref,
                  sum_ref, far_out_ref, slots, rows_a, rows_b, q, row_phase, power, corr, weight):
    slots[0 : 2 * HALF, :] = near_ref[...].astype(F32)
    slots[2 * HALF : 4 * HALF, :] = far_ref[...].astype(F32)

    def fetch(r, rows, k):
        for y in range(k * CH, (k + 1) * CH):
            at = pl.multiple_of(pos_ref[r, y], 2)
            rows[2 * y : 2 * y + 2, :] = slots[pl.ds(at, 2), :]

    def put(r, rows, k):
        for y in range(k * CH, (k + 1) * CH):
            at = pl.multiple_of(pos_ref[r, y], 2)
            sum_ref[pl.ds(at, 2), :] = rows[2 * y : 2 * y + 2, :]

    def images(p, k):
        at = p * 512 + k * CH
        return img_ref[at : at + CH, :], img_ref[at + KY : at + KY + CH, :]

    def score_ref(r, rows, ahead, ahead_rows):
        sums = [jnp.zeros((8, KX), F32) for _ in range(PER)]
        for k in range(KY // CH):
            fetch(ahead, ahead_rows, k)
            re = rows[pl.ds(2 * CH * k, CH, stride=2), :]
            im = rows[pl.ds(2 * CH * k + 1, CH, stride=2), :]
            mag = re * re + im * im
            for p in range(PER):
                a_re, a_im = images(p, k)
                q[pl.ds(pl.multiple_of(r * KY + k * CH, CH), CH), p * 256 : p * 256 + 128] = (re * a_re + im * a_im).astype(BF16)
                q[pl.ds(pl.multiple_of(r * KY + k * CH, CH), CH), p * 256 + 128 : (p + 1) * 256] = (re * a_im - im * a_re).astype(BF16)
                part = sq_ref[p * KY + k * CH : p * KY + (k + 1) * CH, :] * mag
                sums[p] = sums[p] + jnp.sum(part.reshape(CH // 8, 8, KX), axis=0)
        for p in range(PER):
            power[pl.ds(p * REFS + r, 1), :] = jnp.sum(sums[p], axis=0, keepdims=True)

    def forward(t, carry):
        r = 2 * t
        score_ref(r, rows_a, r + 1, rows_b)
        score_ref(r + 1, rows_b, jnp.minimum(r + 2, REFS - 1), rows_a)
        return carry

    for k in range(KY // CH):
        fetch(0, rows_a, k)
    lax.fori_loop(0, REFS // 2, forward, 0)
    for m in range(ROWS // BIG):
        at = slice(m * BIG, (m + 1) * BIG)
        row_phase[at, :] = jnp.dot(q[at, :], fwd_ref[...], preferred_element_type=F32).astype(BF16)
    for r in range(REFS):
        both = jnp.dot(corr_ref[...], row_phase[r * KY : (r + 1) * KY, :], preferred_element_type=F32)
        corr[r * SHIFTS : (r + 1) * SHIFTS, :] = both[:SHIFTS, :128] - both[SHIFTS:, 128:]


    group = lax.shift_right_logical(iota((1, 128), 1), 5)
    noise = jnp.zeros((1, 128), F32)
    totals = jnp.zeros((REFS, 128), F32)
    for p in range(PER):
        noise = jnp.where(group == p, noise_ref[p], noise)
        column = jnp.sum(power[p * REFS : (p + 1) * REFS, :], axis=1, keepdims=True)
        totals = jnp.where(group == p, column, totals)
    score = corr[...].reshape(REFS, SHIFTS, 128) - 0.5 * totals[:, None, :]
    score = score.reshape(REFS * SHIFTS, 128) * noise
    top = jnp.max(score, axis=0, keepdims=True)
    peak = jnp.zeros((1, 128), F32)
    for p in range(PER):
        peak = jnp.where(group == p, jnp.max(jnp.where(group == p, top, -jnp.inf), axis=1, keepdims=True), peak)
    expo = jnp.exp(score - peak)
    lane_sum = jnp.sum(expo, axis=0, keepdims=True)
    norm = jnp.ones((1, 128), F32)
    for p in range(PER):
        norm = jnp.where(group == p, jnp.sum(jnp.where(group == p, lane_sum, 0.0), axis=1, keepdims=True), norm)
    weight[...] = (expo * (1.0 / norm)).astype(BF16)
    sum_ref[...] = jnp.zeros_like(sum_ref)

    def insert_ref(r, rows, behind, behind_rows):
        w = weight[pl.ds(pl.multiple_of(r * SHIFTS, SHIFTS), SHIFTS), :]
        col = jnp.dot(back_ref[...], w, preferred_element_type=F32).astype(BF16)
        col = jnp.concatenate([col[:KY], col[KY:]], axis=1)
        shifted = jnp.dot(col, bwd_ref[...], preferred_element_type=F32).astype(BF16)
        for k in range(KY // CH):
            put(behind, behind_rows, k)
            ss = shifted[k * CH : (k + 1) * CH].astype(F32)
            t_re = t_im = None
            for p in range(PER):
                a_re, a_im = images(p, k)
                s_re = ss[:, p * 256 : p * 256 + 128]
                s_im = ss[:, p * 256 + 128 : (p + 1) * 256]
                u_re = a_re * s_re - a_im * s_im
                u_im = a_re * s_im + a_im * s_re
                t_re = u_re if t_re is None else t_re + u_re
                t_im = u_im if t_im is None else t_im + u_im
            rows[pl.ds(2 * CH * k, CH, stride=2), :] = t_re
            rows[pl.ds(2 * CH * k + 1, CH, stride=2), :] = t_im

    def backward(t, carry):
        r = 2 * t
        insert_ref(r, rows_a, (r + REFS - 1) % REFS, rows_b)
        insert_ref(r + 1, rows_b, r, rows_a)
        return carry

    lax.fori_loop(0, REFS // 2, backward, 0)
    for k in range(KY // CH):
        put(REFS - 1, rows_b, k)
    far_out_ref[...] = sum_ref[2 * HALF : 4 * HALF, :].astype(BF16)


def insert_kernel(mine_ref, got_ref, out_hbm, wide, left, right, out, sems):
    hi_iota = iota((512, 128), 0)
    lo_iota = iota((128, 128), 0)
    sums = jnp.sum(got_ref[...].astype(F32).reshape(8, 24, 128), axis=0)
    wide[...] = sums * (1.0 / math.sqrt(PARTICLES))
    for k in range(CAP):
        vox = mine_ref[k : k + 1, :]
        at = slice(k * 128, (k + 1) * 128)
        left[:, at] = (hi_iota == lax.shift_right_arithmetic(vox, 7)).astype(F32).astype(BF16)
        here = lo_iota == (vox & 127)
        for c in range(2):
            total = wide[2 * k + c : 2 * k + c + 1, :] + wide[12 + 2 * k + c : 12 + 2 * k + c + 1, :]
            first = total.astype(BF16).astype(F32)
            right[c * 256 : c * 256 + 128, at] = jnp.where(here, first, 0.0).astype(BF16)
            right[c * 256 + 128 : c * 256 + 256, at] = jnp.where(here, total - first, 0.0).astype(BF16)
    size = 512 // PIECES
    stores = []
    for m in range(PIECES):
        both = lax.dot_general(
            left[m * size : (m + 1) * size, :], right[...], (((1,), (1,)), ((), ())), preferred_element_type=F32
        )
        for c in range(2):
            out[pl.ds(2 * size * m + c, size, stride=2), :] = (
                both[:, c * 256 : c * 256 + 128] + both[:, c * 256 + 128 : c * 256 + 256]
            )
        at = pl.ds(2 * size * m, 2 * size)
        stores.append(pltpu.make_async_copy(out.at[at, :], out_hbm.at[at, :], sems.at[m]))
        stores[m].start()
    for store in stores:
        store.wait()


def pair_kernel(sums_ref, got_ref, out_ref):
    out_ref[...] = (sums_ref[0 : 2 * HALF, :] + got_ref[...].astype(F32)).astype(BF16)


def line_kernel(got_ref, out_ref):
    total = got_ref[0:192, :].astype(F32)
    for k in range(1, 16):
        total = total + got_ref[k * 192 : (k + 1) * 192, :].astype(F32)
    out_ref[...] = total.astype(BF16)


VM = pl.BlockSpec(memory_space=pltpu.VMEM)
SM = pl.BlockSpec(memory_space=pltpu.SMEM)
ANY = pl.BlockSpec(memory_space=pl.ANY)


def shape(dims, dtype):
    return jax.ShapeDtypeStruct(dims, dtype)


def params():
    return pltpu.CompilerParams(vmem_limit_bytes=VMEM_LIMIT)


def cost(us):
    return pl.CostEstimate(flops=int(us * 1e9), bytes_accessed=int(us * 1e6), transcendentals=0)


def pick_call(me, owner, volume_rows, voxel_rows):
    return pl.pallas_call(
        pick_kernel,
        out_shape=(
            shape((REFS, KY), jnp.int32),
            shape((8, 128), jnp.int32),
            shape((16 * 12, 128), BF16),
        ),
        in_specs=[SM, ANY, ANY, ANY],
        out_specs=(VM, VM, VM),
        scratch_shapes=[
            pltpu.VMEM((REFS, KY), jnp.int32),
            pltpu.VMEM((REFS, KY), jnp.int32),
            pltpu.VMEM((96, 128), F32),
            pltpu.VMEM((1024, 128), BF16),
            pltpu.VMEM((ROWS, KX), jnp.int32),
            pltpu.SemaphoreType.DMA((3,)),
        ],
        compiler_params=pltpu.CompilerParams(vmem_limit_bytes=430 * 128 * 1024),
        name="pick_rows",
    )(me, owner, volume_rows, voxel_rows)


def image_call(defocus, particle_rows):
    return pl.pallas_call(
        image_kernel,
        out_shape=(shape((PER * 512, KX), F32), shape((PER * KY, KX), F32)),
        in_specs=[SM, VM],
        out_specs=(VM, VM),
        scratch_shapes=[pltpu.VMEM((512, KX), F32)],
        compiler_params=params(),
        cost_estimate=cost(4),
        name="ctf_images",
    )(defocus, particle_rows)


def search_call(pos, noise, near, far, img, sq):
    tables = [jnp.asarray(t) for t in phase_constants()]
    return pl.pallas_call(
        search_kernel,
        out_shape=(shape((4 * HALF, KX), F32), shape((2 * HALF, KX), BF16)),
        in_specs=[SM, SM] + [VM] * 8,
        out_specs=(VM, VM),
        scratch_shapes=[
            pltpu.VMEM((4 * HALF, KX), F32),
            pltpu.VMEM((2 * KY, KX), F32),
            pltpu.VMEM((2 * KY, KX), F32),
            pltpu.VMEM((REFS * KY, PER * 2 * KX), BF16),
            pltpu.VMEM((REFS * KY, 2 * PER * SHIFTS), BF16),
            pltpu.VMEM((PER * REFS, KX), F32),
            pltpu.VMEM((REFS * SHIFTS, 128), F32),
            pltpu.VMEM((REFS * SHIFTS, 128), BF16),
        ],
        compiler_params=params(),
        name="shift_search",
    )(pos, noise, near, far, img, sq, *tables)


def small_call(kernel, name, rows, *args):
    return pl.pallas_call(
        kernel,
        out_shape=shape((rows, 128), BF16),
        in_specs=[VM] * len(args),
        out_specs=VM,
        compiler_params=params(),
        name=name,
    )(*args)


def insert_call(mine, got):
    return pl.pallas_call(
        insert_kernel,
        out_shape=shape((1024, 128), F32),
        in_specs=[VM, VM],
        out_specs=ANY,
        scratch_shapes=[
            pltpu.VMEM((24, 128), F32),
            pltpu.VMEM((512, CAP * 128), BF16),
            pltpu.VMEM((512, CAP * 128), BF16),
            pltpu.VMEM((1024, 128), F32),
            pltpu.SemaphoreType.DMA((PIECES,)),
        ],
        compiler_params=params(),
        name="insert_rows",
    )(mine, got)


def local(particles, defocus, inverse_noise, volume, slice_owner, slice_voxel):
    me = lax.axis_index(FINE).astype(jnp.int32).reshape(1)
    volume_rows = volume.reshape(2, 512, 128).transpose(1, 0, 2).reshape(1024, 128)
    pos, mine, compact = pick_call(me, slice_owner, volume_rows, slice_voxel.reshape(ROWS, KX))
    line = lax.all_to_all(compact.reshape(16, CAP, 2, 128), ("zh", "yh"), 0, 0, tiled=True)
    spread = jnp.broadcast_to(line.reshape(1, 96, 2, 128), (16, 96, 2, 128))
    near = lax.all_to_all(spread, ("x", "zl", "yl"), 0, 0, tiled=True).reshape(HALF, 2, 128)
    swap = [(0, 1), (1, 0)]
    far = lax.ppermute(near, "c", swap)
    img, sq = image_call(defocus, particles.reshape(PER * KY * 2, KX))
    sums, far_out = search_call(
        pos, inverse_noise, near.reshape(2 * HALF, 128), far.reshape(2 * HALF, 128), img, sq
    )
    received = lax.ppermute(far_out.reshape(HALF, 2, 128), "c", swap)
    pair = small_call(pair_kernel, "add_core", 2 * HALF, sums, received.reshape(2 * HALF, 128))
    plane = lax.all_to_all(pair.reshape(16, 96, 2, 128), ("x", "zl", "yl"), 0, 0, tiled=True)
    plane = small_call(line_kernel, "add_line", 192, plane.reshape(2 * HALF, 128))
    last = lax.all_to_all(plane.reshape(16, CAP, 2, 128), ("zh", "yh"), 0, 0, tiled=True)
    out = insert_call(mine, last.reshape(192, 128))
    return out.reshape(512, 2, 128).transpose(1, 0, 2).reshape(2, 65536)


def solution(mesh):
    fine = Mesh(mesh.devices.reshape(4, 2, 4, 2, 4, 2), FINE)
    in_specs = (P(FINE, None, None, None), P(FINE), P(FINE), P(None, FINE), P(), P())
    return jax.shard_map(local, mesh=fine, in_specs=in_specs, out_specs=P(None, FINE), check_vma=False)
```

```python
import math

import jax
import jax.numpy as jnp
import ml_dtypes
import numpy as np
from jax import lax
from jax.experimental import pallas as pl
from jax.experimental.pallas import tpu as pltpu
from jax.sharding import Mesh
from jax.sharding import PartitionSpec as P

KY, KX, REFS, SHIFTS, CAP, PER = 256, 128, 8, 32, 6, 4
ROWS = REFS * KY
PARTICLES = 2048
HALF = 1536
BOX = 400
WAVE = 0.0197
AMP = 0.1
VMEM_LIMIT = 40 * 1024 * 1024
FINE = ("zh", "c", "yh", "yl", "x", "zl")
F32 = jnp.float32
BF16 = jnp.bfloat16


def phase_constants():
    shift = np.arange(SHIFTS) - SHIFTS // 2
    fy = np.arange(KY) - KY // 2
    fx = np.arange(KX)
    ang_y = 2.0 * np.pi / BOX * np.mod(fy[:, None] * shift[None, :], BOX)
    ang_x = 2.0 * np.pi / BOX * np.mod(fx[:, None] * shift[None, :], BOX)
    cos_y, sin_y, cos_x, sin_x = np.cos(ang_y), np.sin(ang_y), np.cos(ang_x), np.sin(ang_x)
    fwd = np.zeros((PER, 2, KX, 2, PER, SHIFTS))
    bwd = np.zeros((2, PER, SHIFTS, PER, 2, KX))
    for p in range(PER):
        fwd[p, 0, :, 0, p], fwd[p, 0, :, 1, p] = cos_x, sin_x
        fwd[p, 1, :, 0, p], fwd[p, 1, :, 1, p] = -sin_x, cos_x
        bwd[0, p, :, p, 0], bwd[0, p, :, p, 1] = cos_x.T, sin_x.T
        bwd[1, p, :, p, 0], bwd[1, p, :, p, 1] = -sin_x.T, cos_x.T
    fwd = fwd.reshape(PER * 2 * KX, 2 * PER * SHIFTS)
    bwd = bwd.reshape(2 * PER * SHIFTS, PER * 2 * KX)
    corr = np.concatenate([cos_y.T, sin_y.T], axis=0)
    back = np.concatenate([cos_y, sin_y], axis=0)
    return [a.astype(np.float32).astype(ml_dtypes.bfloat16) for a in (fwd, bwd, corr, back)]


def iota(shape, dim):
    return lax.broadcasted_iota(jnp.int32, shape, dim)


def pick_kernel(me_ref, own_hbm, vol_hbm, vox_hbm, pos_ref, mine_ref, out_ref, owners, slot, stage, table, voxels, sems):
    load_own = pltpu.make_async_copy(own_hbm, owners, sems.at[0])
    load_vox = pltpu.make_async_copy(vox_hbm, voxels, sems.at[1])
    load_vol = pltpu.make_async_copy(vol_hbm, table, sems.at[2])
    load_own.start()
    load_vox.start()
    load_vol.start()
    me = me_ref[0]
    load_own.wait()
    own = owners[...]
    turned = own.astype(F32).T
    cols, here = [], []
    for b in range(ROWS // 128):
        r, h = b // 2, b % 2
        cols.append(jnp.broadcast_to(turned[h * 128 : (h + 1) * 128, r : r + 1], (128, 128)))
        here.append(jnp.broadcast_to(own[r : r + 1, h * 128 : (h + 1) * 128].astype(F32), (128, 128)))
    earlier = iota((128, 128), 0) < iota((128, 128), 1)
    for b in range(ROWS // 128):
        r, h = b // 2, b % 2
        hits = ((cols[b] == here[b]) & earlier).astype(F32)
        for c in range(b):
            hits = hits + (cols[c] == here[b]).astype(F32)
        slot[r : r + 1, h * 128 : (h + 1) * 128] = jnp.sum(hits, axis=0, keepdims=True).astype(jnp.int32)
    slots = slot[...]
    row_id = iota((REFS, KY), 0) * KY + iota((REFS, KY), 1)
    is_me = own == me
    found = [jnp.max(jnp.where(is_me & (slots == k), row_id, -1)) for k in range(CAP)]
    z = lax.shift_right_logical(own, 7)
    y = lax.shift_right_logical(own, 3) & 7
    x = lax.shift_right_logical(own, 1) & 3
    across = ((lax.shift_right_logical(own, 6) ^ lax.shift_right_logical(me, 6)) & 1) * HALF
    pos_ref[...] = 2 * (across + (x * 4 + (own & 1) * 2 + (y & 1)) * (16 * CAP) + (z * 4 + lax.shift_right_logical(y, 1)) * CAP + jnp.minimum(slots, CAP - 1))
    parity = (iota((8, 128), 0) & 1) == 0
    row_pair = lax.shift_right_logical(iota((1024, 128), 0), 1)
    lo_iota = iota((128, 128), 0)
    mine_ref[...] = jnp.full((8, 128), -1, jnp.int32)
    load_vox.wait()
    load_vol.wait()
    for k in range(CAP):
        vox = voxels[pl.ds(jnp.maximum(found[k], 0), 1), :]
        vox = jnp.where(found[k] >= 0, vox, -1)
        mine_ref[k : k + 1, :] = vox
        hi = lax.shift_right_arithmetic(vox, 7)
        onehot = (lo_iota == (vox & 127)).astype(F32).astype(BF16)
        wide = jnp.dot(table[...], onehot, preferred_element_type=F32)
        kept = jnp.where(row_pair == hi, wide, 0.0)
        kept = jnp.sum(kept.reshape(128, 8, 128), axis=0)
        re = jnp.sum(jnp.where(parity, kept, 0.0), axis=0, keepdims=True)
        im = jnp.sum(jnp.where(parity, 0.0, kept), axis=0, keepdims=True)
        for copy in range(8):
            stage[copy * 12 + 2 * k : copy * 12 + 2 * k + 1, :] = re
            stage[copy * 12 + 2 * k + 1 : copy * 12 + 2 * k + 2, :] = im
    block = stage[...].astype(BF16)
    for copy in range(2):
        out_ref[copy * 96 : (copy + 1) * 96, :] = block


def image_kernel(defocus_ref, part_ref, img_ref, sq_ref, wide):
    fy = (iota((KY, KX), 0) - KY // 2).astype(F32)
    fx = iota((KY, KX), 1).astype(F32)
    radius = (fy * fy + fx * fx) / float(BOX * BOX)
    phase0 = math.asin(AMP)
    pi_a = 3.140625
    pi_b = 9.67502593994140625e-4
    pi_c = math.pi - pi_a - pi_b
    coef = [(-1.0) ** k / math.factorial(2 * k + 1) for k in range(7)]
    for p in range(PER):
        wide[...] = part_ref[p * 512 : (p + 1) * 512, :].astype(F32)
        chi = (math.pi * WAVE * defocus_ref[p]) * radius
        whole = jnp.floor(chi * (1.0 / math.pi) + (phase0 / math.pi + 0.5))
        frac = ((chi - whole * pi_a) - whole * pi_b) - (whole * pi_c - phase0)
        half = whole * 0.5
        frac = frac * (1.0 - 4.0 * (half - jnp.floor(half)))
        sq = frac * frac
        poly = jnp.full_like(sq, coef[6])
        for k in range(5, -1, -1):
            poly = poly * sq + coef[k]
        ctf = -(poly * frac)
        sq_ref[p * KY : (p + 1) * KY, :] = ctf * ctf
        img_ref[p * 512 : p * 512 + KY, :] = ctf * wide[pl.ds(0, KY, stride=2), :]
        img_ref[p * 512 + KY : (p + 1) * 512, :] = ctf * wide[pl.ds(1, KY, stride=2), :]


CH = 64


def mul(at, size):
    return at if isinstance(at, int) else pl.multiple_of(at, size)


PIECES = 2


def search_kernel(pos_ref, noise_ref, near_ref, far_ref, img_ref, sq_ref, fwd_ref, bwd_ref, corr_ref, back_ref,
                  sum_ref, far_out_ref, slots, rows_a, rows_b, q, row_phase, power, corr, weight):
    slots[0 : 2 * HALF, :] = near_ref[...].astype(F32)
    slots[2 * HALF : 4 * HALF, :] = far_ref[...].astype(F32)

    def fetch(r, rows, k):
        for y in range(k * CH, (k + 1) * CH):
            at = pl.multiple_of(pos_ref[r, y], 2)
            rows[2 * y : 2 * y + 2, :] = slots[pl.ds(at, 2), :]

    def put(r, rows, k):
        for y in range(k * CH, (k + 1) * CH):
            at = pl.multiple_of(pos_ref[r, y], 2)
            sum_ref[pl.ds(at, 2), :] = rows[2 * y : 2 * y + 2, :]

    def images(p, k):
        at = p * 512 + k * CH
        return img_ref[at : at + CH, :], img_ref[at + KY : at + KY + CH, :]

    def score_ref(r, rows, ahead, ahead_rows):
        sums = [jnp.zeros((8, KX), F32) for _ in range(PER)]
        for k in range(KY // CH):
            fetch(ahead, ahead_rows, k)
            re = rows[pl.ds(2 * CH * k, CH, stride=2), :]
            im = rows[pl.ds(2 * CH * k + 1, CH, stride=2), :]
            mag = re * re + im * im
            for p in range(PER):
                a_re, a_im = images(p, k)
                q[pl.ds(mul(r * KY + k * CH, CH), CH), p * 256 : p * 256 + 128] = (re * a_re + im * a_im).astype(BF16)
                q[pl.ds(mul(r * KY + k * CH, CH), CH), p * 256 + 128 : (p + 1) * 256] = (re * a_im - im * a_re).astype(BF16)
                part = sq_ref[p * KY + k * CH : p * KY + (k + 1) * CH, :] * mag
                sums[p] = sums[p] + jnp.sum(part.reshape(CH // 8, 8, KX), axis=0)
        for p in range(PER):
            power[pl.ds(p * REFS + r, 1), :] = jnp.sum(sums[p], axis=0, keepdims=True)

    def forward(t, carry):
        r = 2 * t
        score_ref(r, rows_a, r + 1, rows_b)
        score_ref(r + 1, rows_b, jnp.minimum(r + 2, REFS - 1), rows_a)
        return carry

    for k in range(KY // CH):
        fetch(0, rows_a, k)
    def turn(start, size):
        at = slice(start, start + size)
        row_phase[at, :] = jnp.dot(q[at, :], fwd_ref[...], preferred_element_type=F32).astype(BF16)

    lax.fori_loop(0, REFS // 4, forward, 0)
    half = REFS // 2
    for r in range(half, REFS):
        buffers = (rows_a, rows_b) if r % 2 == 0 else (rows_b, rows_a)
        turn((r - half) * KY, KY)
        score_ref(r, buffers[0], min(r + 1, REFS - 1), buffers[1])
    turn(half * KY, half * KY)
    for r in range(REFS):
        both = jnp.dot(corr_ref[...], row_phase[r * KY : (r + 1) * KY, :], preferred_element_type=F32)
        corr[r * SHIFTS : (r + 1) * SHIFTS, :] = both[:SHIFTS, :128] - both[SHIFTS:, 128:]


    group = lax.shift_right_logical(iota((1, 128), 1), 5)
    noise = jnp.zeros((1, 128), F32)
    totals = jnp.zeros((REFS, 128), F32)
    for p in range(PER):
        noise = jnp.where(group == p, noise_ref[p], noise)
        column = jnp.sum(power[p * REFS : (p + 1) * REFS, :], axis=1, keepdims=True)
        totals = jnp.where(group == p, column, totals)
    score = corr[...].reshape(REFS, SHIFTS, 128) - 0.5 * totals[:, None, :]
    score = score.reshape(REFS * SHIFTS, 128) * noise
    top = jnp.max(score, axis=0, keepdims=True)
    peak = jnp.zeros((1, 128), F32)
    for p in range(PER):
        peak = jnp.where(group == p, jnp.max(jnp.where(group == p, top, -jnp.inf), axis=1, keepdims=True), peak)
    expo = jnp.exp(score - peak)
    lane_sum = jnp.sum(expo, axis=0, keepdims=True)
    norm = jnp.ones((1, 128), F32)
    for p in range(PER):
        norm = jnp.where(group == p, jnp.sum(jnp.where(group == p, lane_sum, 0.0), axis=1, keepdims=True), norm)
    weight[...] = (expo * (1.0 / norm)).astype(BF16)
    sum_ref[...] = jnp.zeros_like(sum_ref)

    def insert_ref(r, rows, behind, behind_rows):
        w = weight[pl.ds(mul(r * SHIFTS, SHIFTS), SHIFTS), :]
        col = jnp.dot(back_ref[...], w, preferred_element_type=F32).astype(BF16)
        col = jnp.concatenate([col[:KY], col[KY:]], axis=1)
        shifted = jnp.dot(col, bwd_ref[...], preferred_element_type=F32).astype(BF16)
        for k in range(KY // CH):
            put(behind, behind_rows, k)
            ss = shifted[k * CH : (k + 1) * CH].astype(F32)
            t_re = t_im = None
            for p in range(PER):
                a_re, a_im = images(p, k)
                s_re = ss[:, p * 256 : p * 256 + 128]
                s_im = ss[:, p * 256 + 128 : (p + 1) * 256]
                u_re = a_re * s_re - a_im * s_im
                u_im = a_re * s_im + a_im * s_re
                t_re = u_re if t_re is None else t_re + u_re
                t_im = u_im if t_im is None else t_im + u_im
            rows[pl.ds(2 * CH * k, CH, stride=2), :] = t_re
            rows[pl.ds(2 * CH * k + 1, CH, stride=2), :] = t_im

    def backward(t, carry):
        r = 2 * t
        insert_ref(r, rows_a, (r + REFS - 1) % REFS, rows_b)
        insert_ref(r + 1, rows_b, r, rows_a)
        return carry

    lax.fori_loop(0, REFS // 2, backward, 0)
    for k in range(KY // CH):
        put(REFS - 1, rows_b, k)
    far_out_ref[...] = sum_ref[2 * HALF : 4 * HALF, :].astype(BF16)


def insert_kernel(mine_ref, got_ref, out_hbm, wide, left, right, out, sems):
    hi_iota = iota((512, 128), 0)
    lo_iota = iota((128, 128), 0)
    sums = jnp.sum(got_ref[...].astype(F32).reshape(8, 24, 128), axis=0)
    wide[...] = sums * (1.0 / math.sqrt(PARTICLES))
    for k in range(CAP):
        vox = mine_ref[k : k + 1, :]
        at = slice(k * 128, (k + 1) * 128)
        left[:, at] = (hi_iota == lax.shift_right_arithmetic(vox, 7)).astype(F32).astype(BF16)
        here = lo_iota == (vox & 127)
        for c in range(2):
            total = wide[2 * k + c : 2 * k + c + 1, :] + wide[12 + 2 * k + c : 12 + 2 * k + c + 1, :]
            first = total.astype(BF16).astype(F32)
            right[c * 256 : c * 256 + 128, at] = jnp.where(here, first, 0.0).astype(BF16)
            right[c * 256 + 128 : c * 256 + 256, at] = jnp.where(here, total - first, 0.0).astype(BF16)
    size = 512 // PIECES
    stores = []
    for m in range(PIECES):
        both = lax.dot_general(
            left[m * size : (m + 1) * size, :], right[...], (((1,), (1,)), ((), ())), preferred_element_type=F32
        )
        for c in range(2):
            out[pl.ds(2 * size * m + c, size, stride=2), :] = (
                both[:, c * 256 : c * 256 + 128] + both[:, c * 256 + 128 : c * 256 + 256]
            )
        at = pl.ds(2 * size * m, 2 * size)
        stores.append(pltpu.make_async_copy(out.at[at, :], out_hbm.at[at, :], sems.at[m]))
        stores[m].start()
    for store in stores:
        store.wait()


def pair_kernel(sums_ref, got_ref, out_ref):
    out_ref[...] = (sums_ref[0 : 2 * HALF, :] + got_ref[...].astype(F32)).astype(BF16)


def line_kernel(got_ref, out_ref):
    total = got_ref[0:192, :].astype(F32)
    for k in range(1, 16):
        total = total + got_ref[k * 192 : (k + 1) * 192, :].astype(F32)
    out_ref[...] = total.astype(BF16)


VM = pl.BlockSpec(memory_space=pltpu.VMEM)
SM = pl.BlockSpec(memory_space=pltpu.SMEM)
ANY = pl.BlockSpec(memory_space=pl.ANY)


def shape(dims, dtype):
    return jax.ShapeDtypeStruct(dims, dtype)


def params():
    return pltpu.CompilerParams(vmem_limit_bytes=VMEM_LIMIT)


def cost(us):
    return pl.CostEstimate(flops=int(us * 1e9), bytes_accessed=int(us * 1e6), transcendentals=0)


def pick_call(me, owner, volume_rows, voxel_rows):
    return pl.pallas_call(
        pick_kernel,
        out_shape=(
            shape((REFS, KY), jnp.int32),
            shape((8, 128), jnp.int32),
            shape((16 * 12, 128), BF16),
        ),
        in_specs=[SM, ANY, ANY, ANY],
        out_specs=(VM, VM, VM),
        scratch_shapes=[
            pltpu.VMEM((REFS, KY), jnp.int32),
            pltpu.VMEM((REFS, KY), jnp.int32),
            pltpu.VMEM((96, 128), F32),
            pltpu.VMEM((1024, 128), BF16),
            pltpu.VMEM((ROWS, KX), jnp.int32),
            pltpu.SemaphoreType.DMA((3,)),
        ],
        compiler_params=pltpu.CompilerParams(vmem_limit_bytes=430 * 128 * 1024),
        name="pick_rows",
    )(me, owner, volume_rows, voxel_rows)


def image_call(defocus, particle_rows):
    return pl.pallas_call(
        image_kernel,
        out_shape=(shape((PER * 512, KX), F32), shape((PER * KY, KX), F32)),
        in_specs=[SM, VM],
        out_specs=(VM, VM),
        scratch_shapes=[pltpu.VMEM((512, KX), F32)],
        compiler_params=params(),
        cost_estimate=cost(4),
        name="ctf_images",
    )(defocus, particle_rows)


def search_call(pos, noise, near, far, img, sq):
    tables = [jnp.asarray(t) for t in phase_constants()]
    return pl.pallas_call(
        search_kernel,
        out_shape=(shape((4 * HALF, KX), F32), shape((2 * HALF, KX), BF16)),
        in_specs=[SM, SM] + [VM] * 8,
        out_specs=(VM, VM),
        scratch_shapes=[
            pltpu.VMEM((4 * HALF, KX), F32),
            pltpu.VMEM((2 * KY, KX), F32),
            pltpu.VMEM((2 * KY, KX), F32),
            pltpu.VMEM((REFS * KY, PER * 2 * KX), BF16),
            pltpu.VMEM((REFS * KY, 2 * PER * SHIFTS), BF16),
            pltpu.VMEM((PER * REFS, KX), F32),
            pltpu.VMEM((REFS * SHIFTS, 128), F32),
            pltpu.VMEM((REFS * SHIFTS, 128), BF16),
        ],
        compiler_params=params(),
        name="shift_search",
    )(pos, noise, near, far, img, sq, *tables)


def small_call(kernel, name, rows, *args):
    return pl.pallas_call(
        kernel,
        out_shape=shape((rows, 128), BF16),
        in_specs=[VM] * len(args),
        out_specs=VM,
        compiler_params=params(),
        name=name,
    )(*args)


def insert_call(mine, got):
    return pl.pallas_call(
        insert_kernel,
        out_shape=shape((1024, 128), F32),
        in_specs=[VM, VM],
        out_specs=ANY,
        scratch_shapes=[
            pltpu.VMEM((24, 128), F32),
            pltpu.VMEM((512, CAP * 128), BF16),
            pltpu.VMEM((512, CAP * 128), BF16),
            pltpu.VMEM((1024, 128), F32),
            pltpu.SemaphoreType.DMA((PIECES,)),
        ],
        compiler_params=params(),
        name="insert_rows",
    )(mine, got)


def local(particles, defocus, inverse_noise, volume, slice_owner, slice_voxel):
    me = lax.axis_index(FINE).astype(jnp.int32).reshape(1)
    volume_rows = volume.reshape(2, 512, 128).transpose(1, 0, 2).reshape(1024, 128)
    pos, mine, compact = pick_call(me, slice_owner, volume_rows, slice_voxel.reshape(ROWS, KX))
    line = lax.all_to_all(compact.reshape(16, CAP, 2, 128), ("zh", "yh"), 0, 0, tiled=True)
    spread = jnp.broadcast_to(line.reshape(1, 96, 2, 128), (16, 96, 2, 128))
    near = lax.all_to_all(spread, ("x", "zl", "yl"), 0, 0, tiled=True).reshape(HALF, 2, 128)
    swap = [(0, 1), (1, 0)]
    far = lax.ppermute(near, "c", swap)
    img, sq = image_call(defocus, particles.reshape(PER * KY * 2, KX))
    sums, far_out = search_call(
        pos, inverse_noise, near.reshape(2 * HALF, 128), far.reshape(2 * HALF, 128), img, sq
    )
    received = lax.ppermute(far_out.reshape(HALF, 2, 128), "c", swap)
    pair = small_call(pair_kernel, "add_core", 2 * HALF, sums, received.reshape(2 * HALF, 128))
    plane = lax.all_to_all(pair.reshape(16, 96, 2, 128), ("x", "zl", "yl"), 0, 0, tiled=True)
    plane = small_call(line_kernel, "add_line", 192, plane.reshape(2 * HALF, 128))
    last = lax.all_to_all(plane.reshape(16, CAP, 2, 128), ("zh", "yh"), 0, 0, tiled=True)
    out = insert_call(mine, last.reshape(192, 128))
    return out.reshape(512, 2, 128).transpose(1, 0, 2).reshape(2, 65536)


def solution(mesh):
    fine = Mesh(mesh.devices.reshape(4, 2, 4, 2, 4, 2), FINE)
    in_specs = (P(FINE, None, None, None), P(FINE), P(FINE), P(None, FINE), P(), P())
    return jax.shard_map(local, mesh=fine, in_specs=in_specs, out_specs=P(None, FINE), check_vma=False)
```

```python
import math

import jax
import jax.numpy as jnp
import ml_dtypes
import numpy as np
from jax import lax
from jax.experimental import pallas as pl
from jax.experimental.pallas import tpu as pltpu
from jax.sharding import Mesh
from jax.sharding import PartitionSpec as P

KY, KX, REFS, SHIFTS, CAP, PER = 256, 128, 8, 32, 6, 4
ROWS = REFS * KY
PARTICLES = 2048
HALF = 1536
BOX = 400
WAVE = 0.0197
AMP = 0.1
VMEM_LIMIT = 40 * 1024 * 1024
FINE = ("zh", "c", "yh", "yl", "x", "zl")
F32 = jnp.float32
BF16 = jnp.bfloat16


def phase_constants():
    shift = np.arange(SHIFTS) - SHIFTS // 2
    fy = np.arange(KY) - KY // 2
    fx = np.arange(KX)
    ang_y = 2.0 * np.pi / BOX * np.mod(fy[:, None] * shift[None, :], BOX)
    ang_x = 2.0 * np.pi / BOX * np.mod(fx[:, None] * shift[None, :], BOX)
    cos_y, sin_y, cos_x, sin_x = np.cos(ang_y), np.sin(ang_y), np.cos(ang_x), np.sin(ang_x)
    fwd = np.zeros((PER, 2, KX, 2, PER, SHIFTS))
    bwd = np.zeros((2, PER, SHIFTS, PER, 2, KX))
    for p in range(PER):
        fwd[p, 0, :, 0, p], fwd[p, 0, :, 1, p] = cos_x, sin_x
        fwd[p, 1, :, 0, p], fwd[p, 1, :, 1, p] = -sin_x, cos_x
        bwd[0, p, :, p, 0], bwd[0, p, :, p, 1] = cos_x.T, sin_x.T
        bwd[1, p, :, p, 0], bwd[1, p, :, p, 1] = -sin_x.T, cos_x.T
    fwd = fwd.reshape(PER * 2 * KX, 2 * PER * SHIFTS)
    bwd = bwd.reshape(2 * PER * SHIFTS, PER * 2 * KX)
    corr = np.concatenate([cos_y.T, sin_y.T], axis=0)
    back = np.concatenate([cos_y, sin_y], axis=0)
    return [a.astype(np.float32).astype(ml_dtypes.bfloat16) for a in (fwd, bwd, corr, back)]


def iota(shape, dim):
    return lax.broadcasted_iota(jnp.int32, shape, dim)


def pick_kernel(me_ref, own_ref, vol_hbm, vox_hbm, pos_ref, mine_ref, out_ref, slot, stage, table, voxels, sems):
    load_vox = pltpu.make_async_copy(vox_hbm, voxels, sems.at[0])
    load_vol = pltpu.make_async_copy(vol_hbm, table, sems.at[1])
    load_vox.start()
    load_vol.start()
    me = me_ref[0]
    own = own_ref[...]
    turned = own.astype(F32).T
    cols, here = [], []
    for b in range(ROWS // 128):
        r, h = b // 2, b % 2
        cols.append(jnp.broadcast_to(turned[h * 128 : (h + 1) * 128, r : r + 1], (128, 128)))
        here.append(jnp.broadcast_to(own[r : r + 1, h * 128 : (h + 1) * 128].astype(F32), (128, 128)))
    earlier = iota((128, 128), 0) < iota((128, 128), 1)
    for b in range(ROWS // 128):
        r, h = b // 2, b % 2
        hits = ((cols[b] == here[b]) & earlier).astype(F32)
        for c in range(b):
            hits = hits + (cols[c] == here[b]).astype(F32)
        slot[r : r + 1, h * 128 : (h + 1) * 128] = jnp.sum(hits, axis=0, keepdims=True).astype(jnp.int32)
    slots = slot[...]
    row_id = iota((REFS, KY), 0) * KY + iota((REFS, KY), 1)
    is_me = own == me
    found = [jnp.max(jnp.where(is_me & (slots == k), row_id, -1)) for k in range(CAP)]
    z = lax.shift_right_logical(own, 7)
    y = lax.shift_right_logical(own, 3) & 7
    x = lax.shift_right_logical(own, 1) & 3
    across = ((lax.shift_right_logical(own, 6) ^ lax.shift_right_logical(me, 6)) & 1) * HALF
    pos_ref[...] = 2 * (across + (x * 4 + (own & 1) * 2 + (y & 1)) * (16 * CAP) + (z * 4 + lax.shift_right_logical(y, 1)) * CAP + jnp.minimum(slots, CAP - 1))
    parity = (iota((8, 128), 0) & 1) == 0
    row_pair = lax.shift_right_logical(iota((1024, 128), 0), 1)
    lo_iota = iota((128, 128), 0)
    mine_ref[...] = jnp.full((8, 128), -1, jnp.int32)
    load_vox.wait()
    load_vol.wait()
    for k in range(CAP):
        vox = voxels[pl.ds(jnp.maximum(found[k], 0), 1), :]
        vox = jnp.where(found[k] >= 0, vox, -1)
        mine_ref[k : k + 1, :] = vox
        hi = lax.shift_right_arithmetic(vox, 7)
        onehot = (lo_iota == (vox & 127)).astype(F32).astype(BF16)
        wide = jnp.dot(table[...], onehot, preferred_element_type=F32)
        kept = jnp.where(row_pair == hi, wide, 0.0)
        kept = jnp.sum(kept.reshape(128, 8, 128), axis=0)
        re = jnp.sum(jnp.where(parity, kept, 0.0), axis=0, keepdims=True)
        im = jnp.sum(jnp.where(parity, 0.0, kept), axis=0, keepdims=True)
        for copy in range(8):
            stage[copy * 12 + 2 * k : copy * 12 + 2 * k + 1, :] = re
            stage[copy * 12 + 2 * k + 1 : copy * 12 + 2 * k + 2, :] = im
    block = stage[...].astype(BF16)
    for copy in range(2):
        out_ref[copy * 96 : (copy + 1) * 96, :] = block


def image_kernel(defocus_ref, part_ref, img_ref, sq_ref, wide):
    fy = (iota((KY, KX), 0) - KY // 2).astype(F32)
    fx = iota((KY, KX), 1).astype(F32)
    radius = (fy * fy + fx * fx) / float(BOX * BOX)
    phase0 = math.asin(AMP)
    pi_a = 3.140625
    pi_b = 9.67502593994140625e-4
    pi_c = math.pi - pi_a - pi_b
    coef = [(-1.0) ** k / math.factorial(2 * k + 1) for k in range(7)]
    for p in range(PER):
        wide[...] = part_ref[p * 512 : (p + 1) * 512, :].astype(F32)
        chi = (math.pi * WAVE * defocus_ref[p]) * radius
        whole = jnp.floor(chi * (1.0 / math.pi) + (phase0 / math.pi + 0.5))
        frac = ((chi - whole * pi_a) - whole * pi_b) - (whole * pi_c - phase0)
        half = whole * 0.5
        frac = frac * (1.0 - 4.0 * (half - jnp.floor(half)))
        sq = frac * frac
        poly = jnp.full_like(sq, coef[6])
        for k in range(5, -1, -1):
            poly = poly * sq + coef[k]
        ctf = -(poly * frac)
        sq_ref[p * KY : (p + 1) * KY, :] = ctf * ctf
        img_ref[p * 512 : p * 512 + KY, :] = ctf * wide[pl.ds(0, KY, stride=2), :]
        img_ref[p * 512 + KY : (p + 1) * 512, :] = ctf * wide[pl.ds(1, KY, stride=2), :]


CH = 64


def mul(at, size):
    return at if isinstance(at, int) else pl.multiple_of(at, size)


PIECES = 2


def search_kernel(pos_ref, noise_ref, near_ref, far_ref, img_ref, sq_ref, fwd_ref, bwd_ref, corr_ref, back_ref,
                  sum_ref, far_out_ref, slots, rows_a, rows_b, q, row_phase, power, corr, weight):
    slots[0 : 2 * HALF, :] = near_ref[...].astype(F32)
    slots[2 * HALF : 4 * HALF, :] = far_ref[...].astype(F32)

    def fetch(r, rows, k):
        for y in range(k * CH, (k + 1) * CH):
            at = pl.multiple_of(pos_ref[r, y], 2)
            rows[2 * y : 2 * y + 2, :] = slots[pl.ds(at, 2), :]

    def put(r, rows, k):
        for y in range(k * CH, (k + 1) * CH):
            at = pl.multiple_of(pos_ref[r, y], 2)
            sum_ref[pl.ds(at, 2), :] = rows[2 * y : 2 * y + 2, :]

    def images(p, k):
        at = p * 512 + k * CH
        return img_ref[at : at + CH, :], img_ref[at + KY : at + KY + CH, :]

    def score_ref(r, rows, ahead, ahead_rows):
        sums = [jnp.zeros((8, KX), F32) for _ in range(PER)]
        for k in range(KY // CH):
            fetch(ahead, ahead_rows, k)
            re = rows[pl.ds(2 * CH * k, CH, stride=2), :]
            im = rows[pl.ds(2 * CH * k + 1, CH, stride=2), :]
            mag = re * re + im * im
            for p in range(PER):
                a_re, a_im = images(p, k)
                q[pl.ds(mul(r * KY + k * CH, CH), CH), p * 256 : p * 256 + 128] = (re * a_re + im * a_im).astype(BF16)
                q[pl.ds(mul(r * KY + k * CH, CH), CH), p * 256 + 128 : (p + 1) * 256] = (re * a_im - im * a_re).astype(BF16)
                part = sq_ref[p * KY + k * CH : p * KY + (k + 1) * CH, :] * mag
                sums[p] = sums[p] + jnp.sum(part.reshape(CH // 8, 8, KX), axis=0)
        for p in range(PER):
            power[pl.ds(p * REFS + r, 1), :] = jnp.sum(sums[p], axis=0, keepdims=True)

    def forward(t, carry):
        r = 2 * t
        score_ref(r, rows_a, r + 1, rows_b)
        score_ref(r + 1, rows_b, jnp.minimum(r + 2, REFS - 1), rows_a)
        return carry

    for k in range(KY // CH):
        fetch(0, rows_a, k)
    def turn(start, size):
        at = slice(start, start + size)
        row_phase[at, :] = jnp.dot(q[at, :], fwd_ref[...], preferred_element_type=F32).astype(BF16)

    lax.fori_loop(0, REFS // 4, forward, 0)
    half = REFS // 2
    for r in range(half, REFS):
        buffers = (rows_a, rows_b) if r % 2 == 0 else (rows_b, rows_a)
        turn((r - half) * KY, KY)
        score_ref(r, buffers[0], min(r + 1, REFS - 1), buffers[1])
    turn(half * KY, half * KY)
    for r in range(REFS):
        both = jnp.dot(corr_ref[...], row_phase[r * KY : (r + 1) * KY, :], preferred_element_type=F32)
        corr[r * SHIFTS : (r + 1) * SHIFTS, :] = both[:SHIFTS, :128] - both[SHIFTS:, 128:]


    group = lax.shift_right_logical(iota((1, 128), 1), 5)
    noise = jnp.zeros((1, 128), F32)
    totals = jnp.zeros((REFS, 128), F32)
    for p in range(PER):
        noise = jnp.where(group == p, noise_ref[p], noise)
        column = jnp.sum(power[p * REFS : (p + 1) * REFS, :], axis=1, keepdims=True)
        totals = jnp.where(group == p, column, totals)
    score = corr[...].reshape(REFS, SHIFTS, 128) - 0.5 * totals[:, None, :]
    score = score.reshape(REFS * SHIFTS, 128) * noise
    top = jnp.max(score, axis=0, keepdims=True)
    peak = jnp.zeros((1, 128), F32)
    for p in range(PER):
        peak = jnp.where(group == p, jnp.max(jnp.where(group == p, top, -jnp.inf), axis=1, keepdims=True), peak)
    expo = jnp.exp(score - peak)
    lane_sum = jnp.sum(expo, axis=0, keepdims=True)
    norm = jnp.ones((1, 128), F32)
    for p in range(PER):
        norm = jnp.where(group == p, jnp.sum(jnp.where(group == p, lane_sum, 0.0), axis=1, keepdims=True), norm)
    weight[...] = (expo * (1.0 / norm)).astype(BF16)
    sum_ref[...] = jnp.zeros_like(sum_ref)

    def insert_ref(r, rows, behind, behind_rows):
        w = weight[pl.ds(mul(r * SHIFTS, SHIFTS), SHIFTS), :]
        col = jnp.dot(back_ref[...], w, preferred_element_type=F32).astype(BF16)
        col = jnp.concatenate([col[:KY], col[KY:]], axis=1)
        shifted = jnp.dot(col, bwd_ref[...], preferred_element_type=F32).astype(BF16)
        for k in range(KY // CH):
            put(behind, behind_rows, k)
            ss = shifted[k * CH : (k + 1) * CH].astype(F32)
            t_re = t_im = None
            for p in range(PER):
                a_re, a_im = images(p, k)
                s_re = ss[:, p * 256 : p * 256 + 128]
                s_im = ss[:, p * 256 + 128 : (p + 1) * 256]
                u_re = a_re * s_re - a_im * s_im
                u_im = a_re * s_im + a_im * s_re
                t_re = u_re if t_re is None else t_re + u_re
                t_im = u_im if t_im is None else t_im + u_im
            rows[pl.ds(2 * CH * k, CH, stride=2), :] = t_re
            rows[pl.ds(2 * CH * k + 1, CH, stride=2), :] = t_im

    def backward(t, carry):
        r = 2 * t
        insert_ref(r, rows_a, (r + REFS - 1) % REFS, rows_b)
        insert_ref(r + 1, rows_b, r, rows_a)
        return carry

    lax.fori_loop(0, REFS // 2, backward, 0)
    for k in range(KY // CH):
        put(REFS - 1, rows_b, k)
    far_out_ref[...] = sum_ref[2 * HALF : 4 * HALF, :].astype(BF16)


def insert_kernel(mine_ref, got_ref, out_hbm, wide, left, right, out, sems):
    hi_iota = iota((512, 128), 0)
    lo_iota = iota((128, 128), 0)
    sums = jnp.sum(got_ref[...].astype(F32).reshape(8, 24, 128), axis=0)
    wide[...] = sums * (1.0 / math.sqrt(PARTICLES))
    for k in range(CAP):
        vox = mine_ref[k : k + 1, :]
        at = slice(k * 128, (k + 1) * 128)
        left[:, at] = (hi_iota == lax.shift_right_arithmetic(vox, 7)).astype(F32).astype(BF16)
        here = lo_iota == (vox & 127)
        for c in range(2):
            total = wide[2 * k + c : 2 * k + c + 1, :] + wide[12 + 2 * k + c : 12 + 2 * k + c + 1, :]
            first = total.astype(BF16).astype(F32)
            right[c * 256 : c * 256 + 128, at] = jnp.where(here, first, 0.0).astype(BF16)
            right[c * 256 + 128 : c * 256 + 256, at] = jnp.where(here, total - first, 0.0).astype(BF16)
    size = 512 // PIECES
    stores = []
    for m in range(PIECES):
        both = lax.dot_general(
            left[m * size : (m + 1) * size, :], right[...], (((1,), (1,)), ((), ())), preferred_element_type=F32
        )
        for c in range(2):
            out[pl.ds(2 * size * m + c, size, stride=2), :] = (
                both[:, c * 256 : c * 256 + 128] + both[:, c * 256 + 128 : c * 256 + 256]
            )
        at = pl.ds(2 * size * m, 2 * size)
        stores.append(pltpu.make_async_copy(out.at[at, :], out_hbm.at[at, :], sems.at[m]))
        stores[m].start()
    for store in stores:
        store.wait()


def pair_kernel(sums_ref, got_ref, out_ref):
    out_ref[...] = (sums_ref[0 : 2 * HALF, :] + got_ref[...].astype(F32)).astype(BF16)


def line_kernel(got_ref, out_ref):
    total = got_ref[0:192, :].astype(F32)
    for k in range(1, 16):
        total = total + got_ref[k * 192 : (k + 1) * 192, :].astype(F32)
    out_ref[...] = total.astype(BF16)


VM = pl.BlockSpec(memory_space=pltpu.VMEM)
SM = pl.BlockSpec(memory_space=pltpu.SMEM)
ANY = pl.BlockSpec(memory_space=pl.ANY)


def shape(dims, dtype):
    return jax.ShapeDtypeStruct(dims, dtype)


def params():
    return pltpu.CompilerParams(vmem_limit_bytes=VMEM_LIMIT)


def cost(us):
    return pl.CostEstimate(flops=int(us * 1e9), bytes_accessed=int(us * 1e6), transcendentals=0)


def pick_call(me, owner, volume_rows, voxel_rows):
    return pl.pallas_call(
        pick_kernel,
        out_shape=(
            shape((REFS, KY), jnp.int32),
            shape((8, 128), jnp.int32),
            shape((16 * 12, 128), BF16),
        ),
        in_specs=[SM, VM, ANY, ANY],
        out_specs=(VM, VM, VM),
        scratch_shapes=[
            pltpu.VMEM((REFS, KY), jnp.int32),
            pltpu.VMEM((96, 128), F32),
            pltpu.VMEM((1024, 128), BF16),
            pltpu.VMEM((ROWS, KX), jnp.int32),
            pltpu.SemaphoreType.DMA((2,)),
        ],
        compiler_params=pltpu.CompilerParams(vmem_limit_bytes=430 * 128 * 1024),
        name="pick_rows",
    )(me, owner, volume_rows, voxel_rows)


def image_call(defocus, particle_rows):
    return pl.pallas_call(
        image_kernel,
        out_shape=(shape((PER * 512, KX), F32), shape((PER * KY, KX), F32)),
        in_specs=[SM, VM],
        out_specs=(VM, VM),
        scratch_shapes=[pltpu.VMEM((512, KX), F32)],
        compiler_params=params(),
        cost_estimate=cost(4),
        name="ctf_images",
    )(defocus, particle_rows)


def search_call(pos, noise, near, far, img, sq):
    tables = [jnp.asarray(t) for t in phase_constants()]
    return pl.pallas_call(
        search_kernel,
        out_shape=(shape((4 * HALF, KX), F32), shape((2 * HALF, KX), BF16)),
        in_specs=[SM, SM] + [VM] * 8,
        out_specs=(VM, VM),
        scratch_shapes=[
            pltpu.VMEM((4 * HALF, KX), F32),
            pltpu.VMEM((2 * KY, KX), F32),
            pltpu.VMEM((2 * KY, KX), F32),
            pltpu.VMEM((REFS * KY, PER * 2 * KX), BF16),
            pltpu.VMEM((REFS * KY, 2 * PER * SHIFTS), BF16),
            pltpu.VMEM((PER * REFS, KX), F32),
            pltpu.VMEM((REFS * SHIFTS, 128), F32),
            pltpu.VMEM((REFS * SHIFTS, 128), BF16),
        ],
        compiler_params=params(),
        name="shift_search",
    )(pos, noise, near, far, img, sq, *tables)


def small_call(kernel, name, rows, *args):
    return pl.pallas_call(
        kernel,
        out_shape=shape((rows, 128), BF16),
        in_specs=[VM] * len(args),
        out_specs=VM,
        compiler_params=params(),
        name=name,
    )(*args)


def insert_call(mine, got):
    return pl.pallas_call(
        insert_kernel,
        out_shape=shape((1024, 128), F32),
        in_specs=[VM, VM],
        out_specs=ANY,
        scratch_shapes=[
            pltpu.VMEM((24, 128), F32),
            pltpu.VMEM((512, CAP * 128), BF16),
            pltpu.VMEM((512, CAP * 128), BF16),
            pltpu.VMEM((1024, 128), F32),
            pltpu.SemaphoreType.DMA((PIECES,)),
        ],
        compiler_params=params(),
        name="insert_rows",
    )(mine, got)


def local(particles, defocus, inverse_noise, volume, slice_owner, slice_voxel):
    me = lax.axis_index(FINE).astype(jnp.int32).reshape(1)
    volume_rows = volume.reshape(2, 512, 128).transpose(1, 0, 2).reshape(1024, 128)
    pos, mine, compact = pick_call(me, slice_owner, volume_rows, slice_voxel.reshape(ROWS, KX))
    line = lax.all_to_all(compact.reshape(16, CAP, 2, 128), ("zh", "yh"), 0, 0, tiled=True)
    spread = jnp.broadcast_to(line.reshape(1, 96, 2, 128), (16, 96, 2, 128))
    near = lax.all_to_all(spread, ("x", "zl", "yl"), 0, 0, tiled=True).reshape(HALF, 2, 128)
    swap = [(0, 1), (1, 0)]
    far = lax.ppermute(near, "c", swap)
    img, sq = image_call(defocus, particles.reshape(PER * KY * 2, KX))
    sums, far_out = search_call(
        pos, inverse_noise, near.reshape(2 * HALF, 128), far.reshape(2 * HALF, 128), img, sq
    )
    received = lax.ppermute(far_out.reshape(HALF, 2, 128), "c", swap)
    pair = small_call(pair_kernel, "add_core", 2 * HALF, sums, received.reshape(2 * HALF, 128))
    plane = lax.all_to_all(pair.reshape(16, 96, 2, 128), ("x", "zl", "yl"), 0, 0, tiled=True)
    plane = small_call(line_kernel, "add_line", 192, plane.reshape(2 * HALF, 128))
    last = lax.all_to_all(plane.reshape(16, CAP, 2, 128), ("zh", "yh"), 0, 0, tiled=True)
    out = insert_call(mine, last.reshape(192, 128))
    return out.reshape(512, 2, 128).transpose(1, 0, 2).reshape(2, 65536)


def solution(mesh):
    fine = Mesh(mesh.devices.reshape(4, 2, 4, 2, 4, 2), FINE)
    in_specs = (P(FINE, None, None, None), P(FINE), P(FINE), P(None, FINE), P(), P())
    return jax.shard_map(local, mesh=fine, in_specs=in_specs, out_specs=P(None, FINE), check_vma=False)
```
